128 devices in a mesh: freq: 16 (over z, x_hi, core), src: 8 (over y, x_lo).
Axes of the slice: x: 4 (x_hi: 2, x_lo: 2; x = x_hi * 2 + x_lo), y: 4, z: 4, core: 2. Of those that a mesh axis runs over, the one named last changes fastest.
Arguments:
- reflection: bfloat16 [2, 16, 5120, 5120], P(None, 'freq', None, 'src'), may hold values from -0.15625 to 0.15625
- focus_start: bfloat16 [256, 5120, 128], P('freq', 'src'), may hold values from -6 to 6
- onsets: int32 [5120, 128], P('src'), may hold values from 16 to 127
Outputs:
- focus_minus: bfloat16 [256, 5120, 128], P('freq', 'src')
- focus_plus: bfloat16 [256, 5120, 128], P('freq', 'src')
The draws below stay inside these ranges and needn't reach their ends.
All inputs are finite; a program needn't handle non-finite values.
Results may differ from the reference program's by a relative error of at most 0.033.
Values may be sent and summed in bfloat16 or wider, within the bound.
No kernel may reach another device: no remote copies, remote signals or barrier semaphores. Data moves between devices by JAX's collectives and lax.ppermute only.
A program may use at most 128 MiB of HBM per device.

```python
import math
import jax
import jax.numpy as jnp
from jax import lax

X = 5120
NT = 256
FOC = 128
NF = 16


def plant(values, own_key, low, largest):
    dims = values.shape
    spot = [jax.random.randint(jax.random.fold_in(own_key, axis), (), 0, dims[axis]) for axis in range(len(dims))]
    values = values.at[tuple(spot)].set(low)
    longest = dims.index(max(dims))
    spot[longest] = (spot[longest] + 1) % dims[longest]
    return values.at[tuple(spot)].set(largest)


def levels(stream_key, extent, shards, smallest, largest):
    def one(axis_at, blocks):
        draws = jax.random.uniform(jax.random.fold_in(jax.random.fold_in(stream_key, 6), axis_at), (blocks,), jnp.float32, smallest / len(shards), largest / len(shards))
        return jnp.repeat(jnp.exp(draws), extent[axis_at] // blocks).reshape((-1,) + (1,) * (len(extent) - axis_at - 1))

    loudness = one(*shards[0])
    for cut in shards[1:]:
        loudness = loudness * one(*cut)
    return loudness


def noise(own_key, shape, spread, limit, pieces=(), kind=jnp.bfloat16):
    array = jax.random.normal(own_key, shape, jnp.float32) * spread
    if len(pieces) > 0:
        array = levels(own_key, shape, pieces, -0.22, 0.18) * array
    return jnp.clip(array, min=-limit, max=limit).astype(kind)


def setup_inputs(seed: int = 0) -> dict:
    keys = jax.random.split(jax.random.key(seed), 4)
    reflection = noise(keys[0], (2, NF, X, X), (4 * X * NF // NT) ** -0.5, 0.15625, ((1, 16), (3, 8)))
    focus_start = noise(keys[1], (NT, X, FOC), 1.0, 6.0, ((0, 16), (1, 8)))
    onsets = plant(jax.random.randint(keys[2], (X, FOC), NT // 16, NT // 2), jax.random.fold_in(keys[2], 1), NT // 16, (NT // 2) - 1).astype(jnp.int32)
    return {"reflection": reflection, "focus_start": focus_start, "onsets": onsets}


TWO_PI = 2.0 * math.pi


def phase_tables(freq_rows, time_rows, time_count):
    phases = ((freq_rows[:, None] + 1) * time_rows[None, :]) % time_count
    angles = phases.astype(jnp.float32) * (TWO_PI / time_count)
    return jnp.cos(angles).astype(jnp.bfloat16), jnp.sin(angles).astype(jnp.bfloat16)


def forward(signal):
    cosines, sines = phase_tables(jnp.arange(NF, dtype=jnp.int32), jnp.arange(NT, dtype=jnp.int32), NT)
    flattened = signal.astype(jnp.bfloat16).reshape(NT, -1)
    real_part = jnp.dot(cosines, flattened, preferred_element_type=jnp.float32)
    imag_part = -jnp.dot(sines, flattened, preferred_element_type=jnp.float32)
    return jnp.stack([real_part, imag_part], axis=1).reshape(NF, 2, X, FOC).astype(jnp.bfloat16)


def apply_response(reflection, spectra, conj_sign):
    def one_freq(freq_index):
        response = lax.dynamic_index_in_dim(reflection, freq_index, 1, keepdims=False)
        spectrum = lax.dynamic_index_in_dim(spectra, freq_index, 0, keepdims=False)
        real_real = jnp.dot(response[0], spectrum[0], preferred_element_type=jnp.float32)
        imag_imag = jnp.dot(response[1], spectrum[1], preferred_element_type=jnp.float32)
        real_imag = jnp.dot(response[0], spectrum[1], preferred_element_type=jnp.float32)
        imag_real = jnp.dot(response[1], spectrum[0], preferred_element_type=jnp.float32)
        real_part = real_real - conj_sign * imag_imag
        imag_part = real_imag + conj_sign * imag_real
        return jnp.stack([real_part, imag_part]).astype(jnp.bfloat16)

    return lax.map(one_freq, jnp.arange(NF, dtype=jnp.int32))


def inverse(spectra):
    cosines, sines = phase_tables(jnp.arange(NF, dtype=jnp.int32), jnp.arange(NT, dtype=jnp.int32), NT)
    flattened = spectra.reshape(NF, 2, -1)
    real_part = jnp.dot(cosines.T, flattened[:, 0], preferred_element_type=jnp.float32)
    imag_part = jnp.dot(sines.T, flattened[:, 1], preferred_element_type=jnp.float32)
    return ((2.0 / NT) * (real_part - imag_part)).reshape(NT, X, FOC)


def window(signal, onsets):
    time_rows = jnp.arange(NT, dtype=jnp.int32)
    distance = jnp.minimum(time_rows, NT - time_rows)
    kept_mask = distance[:, None, None] < onsets[None]
    return jnp.where(kept_mask, signal, jnp.zeros_like(signal))


def reference(reflection, focus_start, onsets):
    minus_field = window(inverse(apply_response(reflection, forward(focus_start), 1.0)), onsets).astype(jnp.bfloat16)
    update = window(inverse(apply_response(reflection, forward(minus_field), -1.0)), onsets)
    plus_field = (focus_start.astype(jnp.float32) + update).astype(jnp.bfloat16)
    return minus_field, plus_field
```

```python
import functools
import math

import jax
import jax.numpy as jnp
import ml_dtypes
import numpy as np
from jax import lax
from jax.experimental import pallas as pl
from jax.experimental.pallas import tpu as pltpu
from jax.sharding import Mesh
from jax.sharding import PartitionSpec as P

NT = 256
NF = 16
FREQ = ("z", "xh", "core")
SRC = ("y", "xl")
MIB = 1 << 20


def angle_tables():
    phases = ((np.arange(NF)[:, None] + 1) * np.arange(NT)[None, :]) % NT
    angles = phases.astype(np.float32) * np.float32(2.0 * math.pi / NT)
    return np.cos(angles), np.sin(angles)


def forward_table():
    cosines, sines = angle_tables()
    return np.stack([cosines, -sines], axis=1)


def inverse_table():
    cosines, sines = angle_tables()
    return (2.0 / NT) * np.stack([cosines, -sines], axis=1).reshape(2 * NF, NT).T


def spread(table, rows):
    return np.kron(table, np.eye(rows, dtype=np.float32)).astype(ml_dtypes.bfloat16)


def first_weights():
    table = forward_table()
    blocks = []
    for dev in range(16):
        own = np.arange(dev * 16, dev * 16 + 16)
        other = np.arange((dev ^ 1) * 16, (dev ^ 1) * 16 + 16)
        freqs = np.arange(8) * 2 + dev % 2
        part = table[freqs].reshape(16, NT)
        blocks.append(np.stack([spread(part[:, own], 16), spread(part[:, other], 16)]))
    return np.stack(blocks)


def inverse_weights(chunk):
    table = inverse_table()
    return np.stack([spread(table[i : i + chunk], 8) for i in range(0, NT, chunk)])


def forward_weights(chunk):
    table = forward_table().reshape(2 * NF, NT)
    return np.stack([spread(table[:, i : i + chunk], 8) for i in range(0, NT, chunk)])


def dot(a, b):
    return jnp.dot(a, b, preferred_element_type=jnp.float32)


def params(mib=48):
    return pltpu.CompilerParams(vmem_limit_bytes=mib * MIB)


def first_kernel(dev_ref, x_ref, xo_ref, w_ref, out_ref):
    rows = x_ref.shape[1]
    for at in range(0, rows, 16):
        own = x_ref[:, at : at + 16, :].reshape(256, 128)
        other = xo_ref[:, at : at + 16, :].reshape(256, 128)
        part = dot(w_ref[0, 0], own) + dot(w_ref[0, 1], other)
        out_ref[:, :, at : at + 16, :] = part.astype(jnp.bfloat16).reshape(8, 2, 16, 128)


def first_transform(dev, x, xo):
    rows = x.shape[1]
    step = 128
    weights = jnp.asarray(first_weights())
    spec = pl.BlockSpec((16, step, 128), lambda i, d: (0, i, 0))
    return pl.pallas_call(
        first_kernel,
        out_shape=jax.ShapeDtypeStruct((8, 2, rows, 128), jnp.bfloat16),
        grid_spec=pltpu.PrefetchScalarGridSpec(
            num_scalar_prefetch=1,
            grid=(rows // step,),
            in_specs=[spec, spec, pl.BlockSpec((1, 2, 256, 256), lambda i, d: (d[0], 0, 0, 0))],
            out_specs=pl.BlockSpec((8, 2, step, 128), lambda i, d: (0, 0, i, 0)),
        ),
        compiler_params=params(),
        name="first_transform",
    )(dev, x, xo, weights)


def product_kernel(sign, summed, s_ref, r_ref, out_ref, held):
    @pl.when(pl.program_id(0) == 0)
    def _():
        if summed:
            total = s_ref[0].astype(jnp.float32)
            for i in range(1, s_ref.shape[0]):
                total = total + s_ref[i].astype(jnp.float32)
            real, imag = total[0], total[1]
        else:
            real = jnp.concatenate([s_ref[i, 0].astype(jnp.float32) for i in range(16)], axis=0)
            imag = jnp.concatenate([s_ref[i, 1].astype(jnp.float32) for i in range(16)], axis=0)
        depth = real.shape[0]
        held[:depth, :128] = real.astype(jnp.bfloat16)
        held[:depth, 128:] = imag.astype(jnp.bfloat16)
        held[depth:, :128] = (-sign * imag).astype(jnp.bfloat16)
        held[depth:, 128:] = (sign * real).astype(jnp.bfloat16)

    both = jnp.concatenate([r_ref[0, 0], r_ref[1, 0]], axis=1)
    part = dot(both, held[...])
    for g in range(16):
        out_ref[g, 0] = part[g * 40 : g * 40 + 40, :128].astype(jnp.bfloat16)
        out_ref[g, 1] = part[g * 40 : g * 40 + 40, 128:].astype(jnp.bfloat16)


def product(spectra, reflection, sign, summed):
    depth = reflection.shape[3]
    zeros = (0,) * spectra.ndim
    return pl.pallas_call(
        functools.partial(product_kernel, sign, summed),
        out_shape=jax.ShapeDtypeStruct((128, 2, 40, 128), jnp.bfloat16),
        grid=(8,),
        in_specs=[
            pl.BlockSpec(spectra.shape, lambda i: zeros),
            pl.BlockSpec((2, 1, 640, depth), lambda i: (0, 0, i, 0)),
        ],
        out_specs=pl.BlockSpec((16, 2, 40, 128), lambda i: (i, 0, 0, 0)),
        scratch_shapes=[pltpu.VMEM((2 * depth, 256), jnp.bfloat16)],
        compiler_params=params(),
        name="product",
    )(spectra, reflection)


def lanes(rows):
    return jnp.concatenate([rows[:, i : i + 8, :].reshape(-1, 128) for i in range(0, 40, 8)], axis=1)


def unlanes(flat):
    parts = [flat[:, i * 128 : i * 128 + 128].reshape(-1, 8, 128) for i in range(5)]
    return jnp.concatenate(parts, axis=1)


def kept(field, first, onsets):
    chunk = field.shape[0] // 8
    times = first + lax.broadcasted_iota(jnp.int32, (chunk, 8, 128), 0)
    distance = jnp.minimum(times, NT - times)
    parts = []
    for i in range(5):
        piece = field[:, i * 128 : i * 128 + 128].reshape(chunk, 8, 128)
        parts.append(jnp.where(distance < onsets[i * 8 : i * 8 + 8][None], piece, 0.0).reshape(-1, 128))
    return jnp.concatenate(parts, axis=1)


def summed_product(p_ref):
    total = p_ref[0].astype(jnp.float32)
    for i in range(1, 8):
        total = total + p_ref[i].astype(jnp.float32)
    return total.reshape(2 * NF, 40, 128)


def middle_kernel(p_ref, onset_ref, wi_ref, wf_ref, sum_ref, out_ref, acc):
    total = summed_product(p_ref)
    sum_ref[...] = total.astype(jnp.bfloat16)
    flat = lanes(total).astype(jnp.bfloat16)
    onsets = onset_ref[0]
    acc[...] = jnp.zeros_like(acc)

    def body(i, carry):
        field = dot(wi_ref[i], flat)
        minus = kept(field, i * 32, onsets).astype(jnp.bfloat16)
        acc[...] += dot(wf_ref[i], minus)
        return carry

    lax.fori_loop(0, 8, body, 0)
    out_ref[...] = unlanes(acc[...]).astype(jnp.bfloat16).reshape(NF, 2, 40, 128)


def onset_spec():
    return pl.BlockSpec((1, 40, 128), lambda i, d: (d[0], 0, 0))


def whole(shape):
    zeros = (0,) * len(shape)
    return pl.BlockSpec(shape, lambda i, d: zeros)


def middle(dev, parts, onsets):
    wi = jnp.asarray(inverse_weights(32))
    wf = jnp.asarray(forward_weights(32))
    return pl.pallas_call(
        lambda d, *refs: middle_kernel(*refs),
        out_shape=(
            jax.ShapeDtypeStruct((2 * NF, 40, 128), jnp.bfloat16),
            jax.ShapeDtypeStruct((NF, 2, 40, 128), jnp.bfloat16),
        ),
        grid_spec=pltpu.PrefetchScalarGridSpec(
            num_scalar_prefetch=1,
            grid=(1,),
            in_specs=[whole(parts.shape), onset_spec(), whole(wi.shape), whole(wf.shape)],
            out_specs=(whole((2 * NF, 40, 128)), whole((NF, 2, 40, 128))),
            scratch_shapes=[pltpu.VMEM((256, 640), jnp.float32)],
        ),
        compiler_params=params(),
        name="middle",
    )(dev, parts, onsets, wi, wf)


def update_kernel(p_ref, onset_ref, wi_ref, out_ref):
    flat = lanes(summed_product(p_ref)).astype(jnp.bfloat16)
    onsets = onset_ref[0]

    def body(i, carry):
        field = kept(dot(wi_ref[i], flat), i * 32, onsets)
        out_ref[pl.ds(i * 32, 32)] = unlanes(field).astype(jnp.bfloat16)
        return carry

    lax.fori_loop(0, 8, body, 0)


def update_of(dev, parts, onsets):
    wi = jnp.asarray(inverse_weights(32))
    return pl.pallas_call(
        lambda d, *refs: update_kernel(*refs),
        out_shape=jax.ShapeDtypeStruct((NT, 40, 128), jnp.bfloat16),
        grid_spec=pltpu.PrefetchScalarGridSpec(
            num_scalar_prefetch=1,
            grid=(1,),
            in_specs=[whole(parts.shape), onset_spec(), whole(wi.shape)],
            out_specs=whole((NT, 40, 128)),
        ),
        compiler_params=params(),
        name="update_of",
    )(dev, parts, onsets, wi)


def minus_kernel(dev_ref, p_ref, onset_ref, w_ref, out_ref):
    first = dev_ref[0] * 16
    pieces = []
    for g in range(2):
        flat = lanes(p_ref[g].astype(jnp.float32)).astype(jnp.bfloat16)
        pieces.append(unlanes(kept(dot(w_ref[0], flat), first, onset_ref[g])))
    out_ref[...] = jnp.concatenate(pieces, axis=1).astype(jnp.bfloat16)


def minus_output(dev, gathered, onsets):
    weights = jnp.asarray(inverse_weights(16))
    return pl.pallas_call(
        minus_kernel,
        out_shape=jax.ShapeDtypeStruct((16, 640, 128), jnp.bfloat16),
        grid_spec=pltpu.PrefetchScalarGridSpec(
            num_scalar_prefetch=1,
            grid=(8,),
            in_specs=[
                pl.BlockSpec((2, 2 * NF, 40, 128), lambda i, d: (i, 0, 0, 0)),
                pl.BlockSpec((2, 40, 128), lambda i, d: (i, 0, 0)),
                pl.BlockSpec((1, 128, 256), lambda i, d: (d[0], 0, 0)),
            ],
            out_specs=pl.BlockSpec((16, 80, 128), lambda i, d: (0, i, 0)),
        ),
        compiler_params=params(),
        name="minus_output",
    )(dev, gathered, onsets, weights)


def plus_kernel(u_ref, x_ref, out_ref):
    update = jnp.concatenate([u_ref[g].astype(jnp.float32) for g in range(16)], axis=1)
    out_ref[...] = (x_ref[...].astype(jnp.float32) + update).astype(jnp.bfloat16)


def plus_output(update, x):
    step = 4
    return pl.pallas_call(
        plus_kernel,
        out_shape=jax.ShapeDtypeStruct(x.shape, jnp.bfloat16),
        grid=(16 // step,),
        in_specs=[
            pl.BlockSpec((16, step, 40, 128), lambda i: (0, i, 0, 0)),
            pl.BlockSpec((step, 640, 128), lambda i: (i, 0, 0)),
        ],
        out_specs=pl.BlockSpec((step, 640, 128), lambda i: (i, 0, 0)),
        compiler_params=params(),
        name="plus_output",
    )(update, x)


def exchange(x, axes):
    return lax.all_to_all(x, axes, 0, 0, tiled=True)


def local(reflection, focus_start, onsets):
    dev = lax.axis_index(FREQ).astype(jnp.int32).reshape(1)
    onsets = onsets.reshape(16, 40, 128)
    other = lax.ppermute(focus_start, "core", [(0, 1), (1, 0)])
    partial = first_transform(dev, focus_start, other)
    partial = exchange(partial, ("z", "xh"))
    start_parts = exchange(product(partial, reflection, 1.0, True), SRC + FREQ)
    product_start, spectra = middle(dev, start_parts.reshape(8, NF, 2, 40, 128), onsets)
    gathered = lax.all_gather(product_start, FREQ)
    spectra = exchange(spectra, FREQ)
    minus_parts = exchange(product(spectra, reflection, -1.0, False), SRC + FREQ)
    update = update_of(dev, minus_parts.reshape(8, NF, 2, 40, 128), onsets)
    update = exchange(update.reshape(16, 16, 40, 128), FREQ)
    minus_field = minus_output(dev, gathered, onsets)
    return minus_field, plus_output(update, focus_start)


def solution(mesh):
    cut = Mesh(mesh.devices.reshape(4, 2, 2, 4, 2), FREQ + SRC)
    return jax.shard_map(
        local,
        mesh=cut,
        in_specs=(P(None, FREQ, None, SRC), P(FREQ, SRC, None), P(SRC, None)),
        out_specs=(P(FREQ, SRC, None), P(FREQ, SRC, None)),
        check_vma=False,
    )
```

```python
import functools
import math

import jax
import jax.numpy as jnp
import ml_dtypes
import numpy as np
from jax import lax
from jax.experimental import pallas as pl
from jax.experimental.pallas import tpu as pltpu
from jax.sharding import Mesh
from jax.sharding import PartitionSpec as P

NT = 256
NF = 16
FREQ = ("z", "xh", "core")
SRC = ("y", "xl")
MIB = 1 << 20


def angle_tables():
    phases = ((np.arange(NF)[:, None] + 1) * np.arange(NT)[None, :]) % NT
    angles = phases.astype(np.float32) * np.float32(2.0 * math.pi / NT)
    return np.cos(angles), np.sin(angles)


def forward_table():
    cosines, sines = angle_tables()
    return np.stack([cosines, -sines], axis=1)


def inverse_table():
    cosines, sines = angle_tables()
    return (2.0 / NT) * np.stack([cosines, -sines], axis=1).reshape(2 * NF, NT).T


def spread(table, rows):
    return np.kron(table, np.eye(rows, dtype=np.float32)).astype(ml_dtypes.bfloat16)


def place(dev):
    return dev // 4, dev // 2 % 2, dev % 2


def frequency(z, xh, core):
    return (z % 4 * 2 + xh % 2) * 2 + core % 2


def first_weights():
    table = forward_table()
    blocks = []
    for dev in range(16):
        z, xh, core = place(dev)
        own = np.arange(dev * 16, dev * 16 + 16)
        other = np.arange((dev ^ 1) * 16, (dev ^ 1) * 16 + 16)
        freqs = [frequency(z + dz, xh + e, core) for dz in range(4) for e in range(2)]
        part = table[freqs].reshape(16, NT)
        blocks.append(np.stack([spread(part[:, own], 16), spread(part[:, other], 16)]))
    return np.stack(blocks)


def last_weights():
    table = inverse_table().reshape(NT, NF, 2)
    blocks = []
    for dev in range(16):
        z, xh, core = place(dev)
        own = np.arange(dev * 16, dev * 16 + 16)
        freqs = [frequency(z - k, xh + e, core + c) for c in range(2) for e in range(2) for k in range(4)]
        blocks.append(spread(table[own][:, freqs].reshape(16, 2 * NF), 16))
    return np.stack(blocks)


def inverse_weights(chunk):
    table = inverse_table()
    return np.stack([spread(table[i : i + chunk], 8) for i in range(0, NT, chunk)])


def forward_weights(chunk):
    table = forward_table().reshape(2 * NF, NT)
    return np.stack([spread(table[:, i : i + chunk], 8) for i in range(0, NT, chunk)])


def dot(a, b):
    return jnp.dot(a, b, preferred_element_type=jnp.float32)


def params(mib=24):
    return pltpu.CompilerParams(vmem_limit_bytes=mib * MIB)


def cost(flops, moved):
    return pl.CostEstimate(flops=flops, bytes_accessed=moved, transcendentals=0)


HALF = 320


def first_kernel(by_z, dev_ref, x_ref, xo_ref, w_ref, *out_refs):
    rows = x_ref.shape[1]
    for at in range(0, rows, 16):
        own = x_ref[:, at : at + 16, :].reshape(256, 128)
        other = xo_ref[:, at : at + 16, :].reshape(256, 128)
        part = dot(w_ref[0, 0], own) + dot(w_ref[0, 1], other)
        part = part.astype(jnp.bfloat16).reshape(4, 2, 2, 16, 128)
        for i, out_ref in enumerate(out_refs):
            out_ref[:, :, at : at + 16, :] = part[i] if by_z else part[:, i]


def first_transform(dev, x, xo, by_z):
    step = 160
    spec = pl.BlockSpec((16, step, 128), lambda i, d: (0, i, 0))
    count, lead = (4, 2) if by_z else (2, 4)
    return pl.pallas_call(
        functools.partial(first_kernel, by_z),
        out_shape=[jax.ShapeDtypeStruct((lead, 2, HALF, 128), jnp.bfloat16)] * count,
        grid_spec=pltpu.PrefetchScalarGridSpec(
            num_scalar_prefetch=1,
            grid=(HALF // step,),
            in_specs=[spec, spec, pl.BlockSpec((1, 2, 256, 256), lambda i, d: (d[0], 0, 0, 0))],
            out_specs=[pl.BlockSpec((lead, 2, step, 128), lambda i, d: (0, 0, i, 0))] * count,
        ),
        compiler_params=params(),
        cost_estimate=cost(700 << 20, 6 << 20),
        name="first_transform",
    )(dev, x, xo, jnp.asarray(first_weights()))


def total_of(refs):
    total = refs[0][...].astype(jnp.float32)
    for ref in refs[1:]:
        total = total + ref[...].astype(jnp.float32)
    return total


def hold(held, real, imag, sign):
    depth = real.shape[0]
    held[:depth, :128] = real.astype(jnp.bfloat16)
    held[:depth, 128:] = imag.astype(jnp.bfloat16)
    held[depth:, :128] = (-sign * imag).astype(jnp.bfloat16)
    held[depth:, 128:] = (sign * real).astype(jnp.bfloat16)


def start_product_kernel(counts, *refs):
    s_refs, (r_ref, out_ref, held) = refs[: sum(counts)], refs[sum(counts) :]

    @pl.when(pl.program_id(0) == 0)
    def _():
        halves = [total_of(s_refs[: counts[0]]), total_of(s_refs[counts[0] :])]
        real, imag = [jnp.concatenate([h[i] for h in halves], axis=0) for i in range(2)]
        hold(held, real, imag, 1.0)

    both = jnp.concatenate([r_ref[0, 0], r_ref[1, 0]], axis=1)
    part = dot(both, held[...])
    for g in range(out_ref.shape[0]):
        out_ref[g, 0] = part[g * 40 : g * 40 + 40, :128].astype(jnp.bfloat16)
        out_ref[g, 1] = part[g * 40 : g * 40 + 40, 128:].astype(jnp.bfloat16)


def start_product(spectra, counts, reflection):
    depth = reflection.shape[3]
    rows = 1280
    return pl.pallas_call(
        functools.partial(start_product_kernel, counts),
        out_shape=jax.ShapeDtypeStruct((128, 2, 40, 128), jnp.bfloat16),
        grid=(5120 // rows,),
        in_specs=[pl.BlockSpec(s.shape, lambda i, n=s.ndim: (0,) * n) for s in spectra]
        + [pl.BlockSpec((2, 1, rows, depth), lambda i: (0, 0, i, 0))],
        out_specs=pl.BlockSpec((rows // 40, 2, 40, 128), lambda i: (i, 0, 0, 0)),
        scratch_shapes=[pltpu.VMEM((2 * depth, 256), jnp.bfloat16)],
        compiler_params=params(),
        cost_estimate=cost(4 << 30, 18 << 20),
        name="start_product",
    )(*spectra, reflection)


def minus_product_kernel(s_ref, r_ref, out_ref, held):
    @pl.when(pl.program_id(0) == 0)
    def _():
        real, imag = [
            jnp.concatenate([s_ref[i, part].astype(jnp.float32) for i in range(16)], axis=0) for part in range(2)
        ]
        hold(held, real, imag, -1.0)

    both = jnp.concatenate([r_ref[0, 0], r_ref[1, 0]], axis=1)
    part = dot(both, held[...]).astype(jnp.bfloat16)
    for g in range(out_ref.shape[0]):
        for i in range(2):
            out_ref[g, i] = part[g * 640 : g * 640 + 640, i * 128 : i * 128 + 128]


def minus_product(spectra, reflection):
    depth = reflection.shape[3]
    rows = 1280
    return pl.pallas_call(
        minus_product_kernel,
        out_shape=jax.ShapeDtypeStruct((8, 2, 640, 128), jnp.bfloat16),
        grid=(5120 // rows,),
        in_specs=[
            pl.BlockSpec(spectra.shape, lambda i: (0, 0, 0, 0)),
            pl.BlockSpec((2, 1, rows, depth), lambda i: (0, 0, i, 0)),
        ],
        out_specs=pl.BlockSpec((rows // 640, 2, 640, 128), lambda i: (i, 0, 0, 0)),
        scratch_shapes=[pltpu.VMEM((2 * depth, 256), jnp.bfloat16)],
        compiler_params=params(),
        cost_estimate=cost(4 << 30, 18 << 20),
        name="minus_product",
    )(spectra, reflection)


def lanes(rows):
    return jnp.concatenate([rows[:, i : i + 8, :].reshape(-1, 128) for i in range(0, 40, 8)], axis=1)


def unlanes(flat):
    parts = [flat[:, i * 128 : i * 128 + 128].reshape(-1, 8, 128) for i in range(5)]
    return jnp.concatenate(parts, axis=1)


def kept(field, first, onsets):
    chunk = field.shape[0] // 8
    times = first + lax.broadcasted_iota(jnp.int32, (chunk, 8, 128), 0)
    distance = jnp.minimum(times, NT - times)
    parts = []
    for i in range(5):
        piece = field[:, i * 128 : i * 128 + 128].reshape(chunk, 8, 128)
        parts.append(jnp.where(distance < onsets[i * 8 : i * 8 + 8][None], piece, 0.0).reshape(-1, 128))
    return jnp.concatenate(parts, axis=1)


def summed_product(p_ref):
    total = p_ref[0].astype(jnp.float32)
    for i in range(1, 8):
        total = total + p_ref[i].astype(jnp.float32)
    return total.reshape(2 * NF, 40, 128)


def middle_kernel(p_ref, onset_ref, wi_ref, wf_ref, sum_ref, out_ref, acc):
    total = summed_product(p_ref)
    sum_ref[...] = total.astype(jnp.bfloat16)
    flat = lanes(total).astype(jnp.bfloat16)
    onsets = onset_ref[0]
    acc[...] = jnp.zeros_like(acc)

    def body(i, carry):
        field = dot(wi_ref[i], flat)
        minus = kept(field, i * 32, onsets).astype(jnp.bfloat16)
        acc[...] += dot(wf_ref[i], minus)
        return carry

    lax.fori_loop(0, 8, body, 0)
    out_ref[...] = unlanes(acc[...]).astype(jnp.bfloat16).reshape(NF, 2, 40, 128)


def onset_spec():
    return pl.BlockSpec((1, 40, 128), lambda i, d: (d[0], 0, 0))


def whole(shape):
    zeros = (0,) * len(shape)
    return pl.BlockSpec(shape, lambda i, d: zeros)


def middle(dev, parts, onsets):
    wi = jnp.asarray(inverse_weights(32))
    wf = jnp.asarray(forward_weights(32))
    return pl.pallas_call(
        lambda d, *refs: middle_kernel(*refs),
        out_shape=(
            jax.ShapeDtypeStruct((2 * NF, 40, 128), jnp.bfloat16),
            jax.ShapeDtypeStruct((NF, 2, 40, 128), jnp.bfloat16),
        ),
        grid_spec=pltpu.PrefetchScalarGridSpec(
            num_scalar_prefetch=1,
            grid=(1,),
            in_specs=[whole(parts.shape), onset_spec(), whole(wi.shape), whole(wf.shape)],
            out_specs=(whole((2 * NF, 40, 128)), whole((NF, 2, 40, 128))),
            scratch_shapes=[pltpu.VMEM((256, 640), jnp.float32)],
        ),
        compiler_params=params(),
        cost_estimate=cost(2 << 30, 8 << 20),
        name="middle",
    )(dev, parts, onsets, wi, wf)


def minus_kernel(dev_ref, *refs):
    mine, others, onset_ref, w_ref, out_ref = refs[:4], refs[4:8], refs[8], refs[9], refs[10]
    dev = dev_ref[0]
    z, xh, core = lax.div(dev, 4), lax.rem(lax.div(dev, 2), 2), lax.rem(dev, 2)
    for k in range(4):
        for e in range(2):
            chip = lax.rem(z + 4 - k, 4) * 2 + lax.rem(xh + e, 2)
            pieces = []
            for ref, at in ((mine[k], core), (others[k], 1 - core)):
                flat = lanes(ref[e].astype(jnp.float32)).astype(jnp.bfloat16)
                pieces.append(unlanes(kept(dot(w_ref[0], flat), dev * 16, onset_ref[chip * 2 + at])))
            swap = core == 1
            both = [jnp.where(swap, pieces[1], pieces[0]), jnp.where(swap, pieces[0], pieces[1])]
            rows = pl.ds(pl.multiple_of(chip * 80, 16), 80)
            out_ref[:, rows, :] = jnp.concatenate(both, axis=1).astype(jnp.bfloat16)


def minus_output(dev, mine, others, onsets):
    weights = jnp.asarray(inverse_weights(16))
    return pl.pallas_call(
        minus_kernel,
        out_shape=jax.ShapeDtypeStruct((16, 640, 128), jnp.bfloat16),
        grid_spec=pltpu.PrefetchScalarGridSpec(
            num_scalar_prefetch=1,
            grid=(1,),
            in_specs=[whole((2, 2 * NF, 40, 128))] * 8
            + [whole((16, 40, 128)), pl.BlockSpec((1, 128, 256), lambda i, d: (d[0], 0, 0))],
            out_specs=whole((16, 640, 128)),
        ),
        compiler_params=params(),
        cost_estimate=cost(700 << 20, 8 << 20),
        name="minus_output",
    )(dev, *mine, *others, onsets, weights)


def plus_kernel(half, dev_ref, *refs):
    *p_refs, onset_ref, x_ref, w_ref = refs[:-2] if half else refs[:-1]
    out_ref = refs[-1]
    first = dev_ref[0] * 16
    rows = x_ref.shape[1]
    times = first + lax.broadcasted_iota(jnp.int32, (16, 16, 128), 0)
    distance = jnp.minimum(times, NT - times)
    for at in range(0, rows, 32):
        sides = []
        for here in (slice(at, at + 16), slice(at + 16, at + 32)):
            if half:
                flat = [p_refs[c * 4 + k][e, :, here, :] for c in range(2) for e in range(2) for k in range(4)]
            else:
                flat = [p_refs[c * 2 + e][k, :, here, :] for c in range(2) for e in range(2) for k in range(4)]
            sides.append(jnp.concatenate([piece.reshape(32, 128) for piece in flat], axis=0))
        field = dot(w_ref[0], jnp.concatenate(sides, axis=1))
        for i in range(2):
            here = slice(at + i * 16, at + i * 16 + 16)
            side = field[:, i * 128 : i * 128 + 128].reshape(16, 16, 128)
            update = jnp.where(distance < onset_ref[here][None], side, 0.0)
            out_ref[:, here, :] = (x_ref[:, here, :].astype(jnp.float32) + update).astype(jnp.bfloat16)


def plus_output(dev, half, parts, onsets, x, held):
    step = 64
    start = half * HALF // step
    weights = jnp.asarray(last_weights())
    lead = 2 if half else 4
    time_spec = pl.BlockSpec((16, step, 128), lambda i, d: (0, i + start, 0))
    operands = [dev, *parts, onsets, x, weights] + ([held] if half else [])
    return pl.pallas_call(
        functools.partial(plus_kernel, half),
        out_shape=jax.ShapeDtypeStruct(x.shape, jnp.bfloat16),
        grid_spec=pltpu.PrefetchScalarGridSpec(
            num_scalar_prefetch=1,
            grid=(HALF // step,),
            in_specs=[pl.BlockSpec((lead, 2, step, 128), lambda i, d: (0, 0, i, 0))] * len(parts)
            + [
                pl.BlockSpec((step, 128), lambda i, d: (i + start, 0)),
                time_spec,
                pl.BlockSpec((1, 256, 512), lambda i, d: (d[0], 0, 0)),
            ]
            + ([pl.BlockSpec(memory_space=pl.ANY)] if half else []),
            out_specs=time_spec,
        ),
        input_output_aliases={len(operands) - 1: 0} if half else {},
        compiler_params=params(),
        cost_estimate=cost(700 << 20, 6 << 20),
        name="plus_output",
    )(*operands)


def exchange(x, axes):
    return lax.all_to_all(x, axes, 0, 0, tiled=True)


def along(x, axis, step):
    size = lax.axis_size(axis)
    return lax.ppermute(x, axis, [(i, (i + step) % size) for i in range(size)])


def add(*arrays):
    total = arrays[0].astype(jnp.float32)
    for array in arrays[1:]:
        total = total + array.astype(jnp.float32)
    return total.astype(jnp.bfloat16)


STEPS = (2, 1, 3)


def start_spectra(dev, x):
    xa, xb = x[:, :HALF], x[:, HALF:]
    xoa, xob = along(xa, "core", 1), along(xb, "core", 1)
    a_got = around(first_transform(dev, xa, xoa, True), "z")
    b_own, b_send = first_transform(dev, xb, xob, False)
    b_got = along(b_send, "xh", 1)
    a_got, b_got = together(a_got, b_got)
    a_keep, a_pass = [add(*[got[e] for got in a_got]) for e in range(2)]
    b_parts = around([add(b_own[k], b_got[k]) for k in range(4)], "z")
    return [a_keep, along(a_pass, "xh", 1)] + b_parts


def around(parts, axis):
    got = {k: along(parts[k], axis, k) for k in STEPS}
    return [parts[0], got[1], got[2], got[3]]


def together(*groups):
    return lax.optimization_barrier(groups)


def local(reflection, focus_start, onsets):
    dev = lax.axis_index(FREQ).astype(jnp.int32).reshape(1)
    blocks = onsets.reshape(16, 40, 128)
    spectra = start_spectra(dev, focus_start)
    start_parts = exchange(start_product(spectra, (2, 4), reflection), SRC + FREQ)
    summed, spectra = middle(dev, start_parts.reshape(8, NF, 2, 40, 128), blocks)
    spectra, far = together(exchange(spectra, FREQ), along(summed, "xh", 1))
    parts, near = together(minus_product(spectra, reflection), jnp.stack([summed, far]))
    parts, mine = together(exchange(parts, SRC), around([near] * 4, "z"))

    total = parts.astype(jnp.float32).sum(0).astype(jnp.bfloat16)
    a, b = total[:, :HALF], total[:, HALF:]
    b_far, a_near = along(b, "xh", 1), around([a] * 4, "z")
    others = [along(v, "core", 1) for v in mine]
    b_far, a_near = together(b_far, a_near)
    a_near, b_near = jnp.stack(a_near), jnp.stack([b, b_far])
    a_far, b_all = together(along(a_near, "xh", 1), around([b_near] * 4, "z"))
    minus_field = minus_output(dev, mine, others, blocks)
    a_all, b_all = [a_near, a_far], list(b_all)
    a_all = a_all + [along(v, "core", 1) for v in a_all]
    b_all = b_all + [along(v, "core", 1) for v in b_all]
    plus_field = plus_output(dev, 0, a_all, onsets, focus_start, None)
    plus_field = plus_output(dev, 1, b_all, onsets, focus_start, plus_field)
    return minus_field, plus_field


def solution(mesh):
    cut = Mesh(mesh.devices.reshape(4, 2, 2, 4, 2), FREQ + SRC)
    return jax.shard_map(
        local,
        mesh=cut,
        in_specs=(P(None, FREQ, None, SRC), P(FREQ, SRC, None), P(SRC, None)),
        out_specs=(P(FREQ, SRC, None), P(FREQ, SRC, None)),
        check_vma=False,
    )
```

```python
import functools
import math

import jax
import jax.numpy as jnp
import ml_dtypes
import numpy as np
from jax import lax
from jax.experimental import pallas as pl
from jax.experimental.pallas import tpu as pltpu
from jax.sharding import Mesh
from jax.sharding import PartitionSpec as P

NT = 256
NF = 16
FREQ = ("z", "xh", "core")
SRC = ("y", "xl")
MIB = 1 << 20


def angle_tables():
    phases = ((np.arange(NF)[:, None] + 1) * np.arange(NT)[None, :]) % NT
    angles = phases.astype(np.float32) * np.float32(2.0 * math.pi / NT)
    return np.cos(angles), np.sin(angles)


def forward_table():
    cosines, sines = angle_tables()
    return np.stack([cosines, -sines], axis=1)


def inverse_table():
    cosines, sines = angle_tables()
    return (2.0 / NT) * np.stack([cosines, -sines], axis=1).reshape(2 * NF, NT).T


def spread(table, rows):
    return np.kron(table, np.eye(rows, dtype=np.float32)).astype(ml_dtypes.bfloat16)


def place(dev):
    return dev // 4, dev // 2 % 2, dev % 2


def frequency(z, xh, core):
    return (z % 4 * 2 + xh % 2) * 2 + core % 2


def first_weights():
    table = forward_table()
    blocks = []
    for dev in range(16):
        z, xh, core = place(dev)
        own = np.arange(dev * 16, dev * 16 + 16)
        other = np.arange((dev ^ 1) * 16, (dev ^ 1) * 16 + 16)
        freqs = [frequency(z + dz, xh + e, core) for dz in range(4) for e in range(2)]
        part = table[freqs].reshape(16, NT)
        blocks.append(spread(part[:, np.concatenate([own, other])], 16))
    return np.stack(blocks)


def last_weights():
    table = inverse_table().reshape(NT, NF, 2)
    blocks = []
    for dev in range(16):
        z, xh, core = place(dev)
        own = np.arange(dev * 16, dev * 16 + 16)
        freqs = [frequency(z - k, xh + e, core + c) for c in range(2) for e in range(2) for k in range(4)]
        blocks.append(spread(table[own][:, freqs].reshape(16, 2 * NF), 16))
    return np.stack(blocks)


def inverse_weights(chunk):
    table = inverse_table()
    return np.stack([spread(table[i : i + chunk], 8) for i in range(0, NT, chunk)])


def forward_weights(chunk):
    table = forward_table().reshape(2 * NF, NT)
    return np.stack([spread(table[:, i : i + chunk], 8) for i in range(0, NT, chunk)])


def dot(a, b):
    return jnp.dot(a, b, preferred_element_type=jnp.float32)


def params(mib=16):
    return pltpu.CompilerParams(vmem_limit_bytes=mib * MIB)


def cost(flops, moved):
    return pl.CostEstimate(flops=flops, bytes_accessed=moved, transcendentals=0)


HALF = 320


def of_device(table, dev):
    return lax.dynamic_index_in_dim(jnp.asarray(table), dev[0], 0, keepdims=False)


def first_kernel(by_z, x_ref, xo_ref, w_ref, *out_refs):
    rows = x_ref.shape[1]
    for at in range(0, rows, 32):
        sides = []
        for here in (slice(at, at + 16), slice(at + 16, at + 32)):
            both = [x_ref[:, here, :].reshape(256, 128), xo_ref[:, here, :].reshape(256, 128)]
            sides.append(jnp.concatenate(both, axis=0))
        both = dot(w_ref[...], jnp.concatenate(sides, axis=1)).astype(jnp.bfloat16)
        for side in range(2):
            part = both[:, side * 128 : side * 128 + 128].reshape(4, 2, 2, 16, 128)
            here = slice(at + side * 16, at + side * 16 + 16)
            for i, out_ref in enumerate(out_refs):
                out_ref[:, :, here, :] = part[i] if by_z else part[:, i]


def copy_kernel(x_ref, out_ref):
    out_ref[...] = x_ref[...]


def copied(x):
    spec = pl.BlockSpec((x.shape[0] // 4,) + x.shape[1:], lambda i: (i, 0, 0))
    return pl.pallas_call(
        copy_kernel,
        out_shape=jax.ShapeDtypeStruct(x.shape, x.dtype),
        grid=(4,),
        in_specs=[spec],
        out_specs=spec,
        compiler_params=params(),
        cost_estimate=cost(0, 6 << 20),
        name="copied",
    )(x)


def first_transform(weights, x, xo, half, by_z):
    step = 160
    start = half * HALF // step
    spec = pl.BlockSpec((16, step, 128), lambda i: (0, i + start, 0))
    count, lead = (4, 2) if by_z else (2, 4)
    return pl.pallas_call(
        functools.partial(first_kernel, by_z),
        out_shape=[jax.ShapeDtypeStruct((lead, 2, HALF, 128), jnp.bfloat16)] * count,
        grid=(HALF // step,),
        in_specs=[spec, spec, pl.BlockSpec((256, 512), lambda i: (0, 0))],
        out_specs=[pl.BlockSpec((lead, 2, step, 128), lambda i: (0, 0, i, 0))] * count,
        compiler_params=params(),
        cost_estimate=cost(700 << 20, 6 << 20),
        name="first_transform",
    )(x, xo, weights)


def total_of(refs):
    total = refs[0][...].astype(jnp.float32)
    for ref in refs[1:]:
        total = total + ref[...].astype(jnp.float32)
    return total


def hold(held, real, imag, sign):
    depth = real.shape[0]
    held[:depth, :128] = real.astype(jnp.bfloat16)
    held[:depth, 128:] = imag.astype(jnp.bfloat16)
    held[depth:, :128] = (-sign * imag).astype(jnp.bfloat16)
    held[depth:, 128:] = (sign * real).astype(jnp.bfloat16)


def start_product_kernel(counts, *refs):
    s_refs, (r_ref, out_ref, held) = refs[: sum(counts)], refs[sum(counts) :]

    @pl.when(pl.program_id(0) == 0)
    def _():
        halves = [total_of(s_refs[: counts[0]]), total_of(s_refs[counts[0] :])]
        real, imag = [jnp.concatenate([h[i] for h in halves], axis=0) for i in range(2)]
        hold(held, real, imag, 1.0)

    both = jnp.concatenate([r_ref[0, 0], r_ref[1, 0]], axis=1)
    part = dot(both, held[...])
    for g in range(out_ref.shape[0]):
        out_ref[g, 0] = part[g * 40 : g * 40 + 40, :128].astype(jnp.bfloat16)
        out_ref[g, 1] = part[g * 40 : g * 40 + 40, 128:].astype(jnp.bfloat16)


def start_product(spectra, counts, reflection):
    depth = reflection.shape[3]
    rows = 1280
    return pl.pallas_call(
        functools.partial(start_product_kernel, counts),
        out_shape=jax.ShapeDtypeStruct((128, 2, 40, 128), jnp.bfloat16),
        grid=(5120 // rows,),
        in_specs=[pl.BlockSpec(s.shape, lambda i, n=s.ndim: (0,) * n) for s in spectra]
        + [pl.BlockSpec((2, 1, rows, depth), lambda i: (0, 0, i, 0))],
        out_specs=pl.BlockSpec((rows // 40, 2, 40, 128), lambda i: (i, 0, 0, 0)),
        scratch_shapes=[pltpu.VMEM((2 * depth, 256), jnp.bfloat16)],
        compiler_params=params(),
        cost_estimate=cost(4 << 30, 18 << 20),
        name="start_product",
    )(*spectra, reflection)


def minus_product_kernel(s_ref, r_ref, out_ref, held):
    @pl.when(pl.program_id(0) == 0)
    def _():
        real, imag = [
            jnp.concatenate([s_ref[i, part].astype(jnp.float32) for i in range(16)], axis=0) for part in range(2)
        ]
        hold(held, real, imag, -1.0)

    both = jnp.concatenate([r_ref[0, 0], r_ref[1, 0]], axis=1)
    part = dot(both, held[...]).astype(jnp.bfloat16)
    for g in range(out_ref.shape[0]):
        for i in range(2):
            out_ref[g, i] = part[g * 640 : g * 640 + 640, i * 128 : i * 128 + 128]


def minus_product(spectra, reflection):
    depth = reflection.shape[3]
    rows = 1280
    return pl.pallas_call(
        minus_product_kernel,
        out_shape=pltpu.HBM((8, 2, 640, 128), jnp.bfloat16),
        grid=(5120 // rows,),
        in_specs=[
            pl.BlockSpec(spectra.shape, lambda i: (0, 0, 0, 0)),
            pl.BlockSpec((2, 1, rows, depth), lambda i: (0, 0, i, 0)),
        ],
        out_specs=pl.BlockSpec((rows // 640, 2, 640, 128), lambda i: (i, 0, 0, 0)),
        scratch_shapes=[pltpu.VMEM((2 * depth, 256), jnp.bfloat16)],
        compiler_params=params(),
        cost_estimate=cost(4 << 30, 18 << 20),
        name="minus_product",
    )(spectra, reflection)


def sum_kernel(p_ref, a_ref, b_ref):
    total = p_ref[0].astype(jnp.float32)
    for i in range(1, 8):
        total = total + p_ref[i].astype(jnp.float32)
    total = total.astype(jnp.bfloat16)
    a_ref[...] = total[:, :HALF]
    b_ref[...] = total[:, HALF:]


def summed_halves(parts):
    return pl.pallas_call(
        sum_kernel,
        out_shape=[jax.ShapeDtypeStruct((2, HALF, 128), jnp.bfloat16)] * 2,
        grid=(2,),
        in_specs=[pl.BlockSpec((8, 1, 640, 128), lambda i: (0, i, 0, 0))],
        out_specs=[pl.BlockSpec((1, HALF, 128), lambda i: (i, 0, 0))] * 2,
        compiler_params=params(),
        cost_estimate=cost(1 << 20, 3 << 20),
        name="summed_halves",
    )(parts)


def lanes(rows):
    return jnp.concatenate([rows[:, i : i + 8, :].reshape(-1, 128) for i in range(0, 40, 8)], axis=1)


def unlanes(flat):
    parts = [flat[:, i * 128 : i * 128 + 128].reshape(-1, 8, 128) for i in range(5)]
    return jnp.concatenate(parts, axis=1)


def kept(field, first, onsets):
    chunk = field.shape[0] // 8
    times = first + lax.broadcasted_iota(jnp.int32, (chunk, 8, 128), 0)
    distance = jnp.minimum(times, NT - times)
    parts = []
    for i in range(5):
        piece = field[:, i * 128 : i * 128 + 128].reshape(chunk, 8, 128)
        parts.append(jnp.where(distance < onsets[i * 8 : i * 8 + 8][None], piece, 0.0).reshape(-1, 128))
    return jnp.concatenate(parts, axis=1)


def summed_product(p_ref):
    total = p_ref[0].astype(jnp.float32)
    for i in range(1, 8):
        total = total + p_ref[i].astype(jnp.float32)
    return total.reshape(2 * NF, 40, 128)


def middle_kernel(p_ref, onset_ref, wi_ref, wf_ref, sum_ref, out_ref, acc):
    total = summed_product(p_ref)
    sum_ref[...] = total.astype(jnp.bfloat16)
    flat = lanes(total).astype(jnp.bfloat16)
    onsets = onset_ref[0]
    acc[...] = jnp.zeros_like(acc)

    def body(i, carry):
        field = dot(wi_ref[i], flat)
        minus = kept(field, i * 64, onsets).astype(jnp.bfloat16)
        acc[...] += dot(wf_ref[i], minus)
        return carry

    lax.fori_loop(0, 4, body, 0)
    out_ref[...] = unlanes(acc[...]).astype(jnp.bfloat16).reshape(NF, 2, 40, 128)


def onset_spec():
    return pl.BlockSpec((1, 40, 128), lambda i, d: (d[0], 0, 0))


def whole(shape):
    zeros = (0,) * len(shape)
    return pl.BlockSpec(shape, lambda i, d: zeros)


def middle(dev, parts, onsets):
    wi = jnp.asarray(inverse_weights(64))
    wf = jnp.asarray(forward_weights(64))
    return pl.pallas_call(
        lambda d, *refs: middle_kernel(*refs),
        out_shape=(
            jax.ShapeDtypeStruct((2 * NF, 40, 128), jnp.bfloat16),
            jax.ShapeDtypeStruct((NF, 2, 40, 128), jnp.bfloat16),
        ),
        grid_spec=pltpu.PrefetchScalarGridSpec(
            num_scalar_prefetch=1,
            grid=(1,),
            in_specs=[whole(parts.shape), onset_spec(), whole(wi.shape), whole(wf.shape)],
            out_specs=(whole((2 * NF, 40, 128)), whole((NF, 2, 40, 128))),
            scratch_shapes=[pltpu.VMEM((256, 640), jnp.float32)],
        ),
        compiler_params=params(),
        cost_estimate=cost(2 << 30, 8 << 20),
        name="middle",
    )(dev, parts, onsets, wi, wf)


def minus_kernel(dev_ref, *refs):
    p_refs, onset_ref, w_ref, out_ref = refs[:8], refs[8], refs[9], refs[10]
    dev = dev_ref[0]
    z, xh, core = lax.div(dev, 4), lax.rem(lax.div(dev, 2), 2), lax.rem(dev, 2)
    for k in range(4):
        for e in range(2):
            chip = lax.rem(z + 4 - k, 4) * 2 + lax.rem(xh + e, 2)
            pieces = []
            for c, at in ((0, core), (1, 1 - core)):
                flat = lanes(p_refs[c * 4 + k][e].astype(jnp.float32)).astype(jnp.bfloat16)
                pieces.append(unlanes(kept(dot(w_ref[...], flat), dev * 16, onset_ref[chip * 2 + at])))
            swap = core == 1
            both = [jnp.where(swap, pieces[1], pieces[0]), jnp.where(swap, pieces[0], pieces[1])]
            rows = pl.ds(pl.multiple_of(chip * 80, 16), 80)
            out_ref[:, rows, :] = jnp.concatenate(both, axis=1).astype(jnp.bfloat16)


def minus_output(dev, parts, onsets, weights):
    return pl.pallas_call(
        minus_kernel,
        out_shape=jax.ShapeDtypeStruct((16, 640, 128), jnp.bfloat16),
        grid_spec=pltpu.PrefetchScalarGridSpec(
            num_scalar_prefetch=1,
            grid=(1,),
            in_specs=[whole((2, 2 * NF, 40, 128))] * 8
            + [whole((16, 40, 128)), whole((128, 256))],
            out_specs=whole((16, 640, 128)),
        ),
        compiler_params=params(),
        cost_estimate=cost(700 << 20, 8 << 20),
        name="minus_output",
    )(dev, *parts, onsets, weights)


def plus_kernel(half, dev_ref, *refs):
    *p_refs, onset_ref, x_ref, w_ref = refs[:-2] if half else refs[:-1]
    out_ref = refs[-1]
    first = dev_ref[0] * 16
    rows = x_ref.shape[1]
    times = first + lax.broadcasted_iota(jnp.int32, (16, 16, 128), 0)
    distance = jnp.minimum(times, NT - times)
    for at in range(0, rows, 32):
        sides = []
        for here in (slice(at, at + 16), slice(at + 16, at + 32)):
            if half:
                flat = [p_refs[c * 4 + k][e, :, here, :] for c in range(2) for e in range(2) for k in range(4)]
            else:
                flat = [p_refs[c * 2 + e][k, :, here, :] for c in range(2) for e in range(2) for k in range(4)]
            sides.append(jnp.concatenate([piece.reshape(32, 128) for piece in flat], axis=0))
        field = dot(w_ref[...], jnp.concatenate(sides, axis=1))
        for i in range(2):
            here = slice(at + i * 16, at + i * 16 + 16)
            side = field[:, i * 128 : i * 128 + 128].reshape(16, 16, 128)
            update = jnp.where(distance < onset_ref[here][None], side, 0.0)
            out_ref[:, here, :] = (x_ref[:, here, :].astype(jnp.float32) + update).astype(jnp.bfloat16)


def plus_output(dev, half, parts, onsets, x, weights, held):
    step = 160
    start = half * HALF // step
    lead = 2 if half else 4
    time_spec = pl.BlockSpec((16, step, 128), lambda i, d: (0, i + start, 0))
    operands = [dev, *parts, onsets, x, weights] + ([held] if half else [])
    return pl.pallas_call(
        functools.partial(plus_kernel, half),
        out_shape=jax.ShapeDtypeStruct(x.shape, jnp.bfloat16),
        grid_spec=pltpu.PrefetchScalarGridSpec(
            num_scalar_prefetch=1,
            grid=(HALF // step,),
            in_specs=[pl.BlockSpec((lead, 2, step, 128), lambda i, d: (0, 0, i, 0))] * len(parts)
            + [
                pl.BlockSpec((step, 128), lambda i, d: (i + start, 0)),
                time_spec,
                whole((256, 512)),
            ]
            + ([pl.BlockSpec(memory_space=pl.ANY)] if half else []),
            out_specs=time_spec,
        ),
        input_output_aliases={len(operands) - 1: 0} if half else {},
        compiler_params=params(),
        cost_estimate=cost(700 << 20, 6 << 20),
        name="plus_output",
    )(*operands)


def exchange(x, axes):
    return lax.all_to_all(x, axes, 0, 0, tiled=True)


def along(x, axis, step):
    size = lax.axis_size(axis)
    return lax.ppermute(x, axis, [(i, (i + step) % size) for i in range(size)])


def add(*arrays):
    total = arrays[0].astype(jnp.float32)
    for array in arrays[1:]:
        total = total + array.astype(jnp.float32)
    return total.astype(jnp.bfloat16)


STEPS = (2, 1, 3)


def start_spectra(dev, x):
    weights = of_device(first_weights(), dev)
    xo = along(x, "core", 1)
    x = copied(x)
    a_send = first_transform(weights, x, xo, 0, True)
    a_send, xo = together(a_send, xo)
    a_got = around(a_send, "z")
    b_own, b_send = first_transform(weights, x, xo, 1, False)
    b_got = along(b_send, "xh", 1)
    a_got, b_got = together(a_got, b_got)
    a_keep, a_pass = [add(*[got[e] for got in a_got]) for e in range(2)]
    b_parts = around([add(b_own[k], b_got[k]) for k in range(4)], "z")
    return [a_keep, along(a_pass, "xh", 1)] + b_parts


def around(parts, axis):
    got = {k: along(parts[k], axis, k) for k in STEPS}
    return [parts[0], got[1], got[2], got[3]]


def rest_of(near):
    mine = around([near] * 4, "z")
    return mine, [along(v, "core", 1) for v in mine[:3]]


def together(*groups):
    return lax.optimization_barrier(groups)


def local(reflection, focus_start, onsets):
    dev = lax.axis_index(FREQ).astype(jnp.int32).reshape(1)
    blocks = onsets.reshape(16, 40, 128)
    spectra = start_spectra(dev, focus_start)
    start_parts = exchange(start_product(spectra, (2, 4), reflection), SRC + FREQ)
    summed, spectra = middle(dev, start_parts.reshape(8, NF, 2, 40, 128), blocks)
    spectra, far = together(exchange(spectra, FREQ), along(summed, "xh", 1))
    parts, near = together(minus_product(spectra, reflection), jnp.stack([summed, far]))
    parts, mine, others = together(exchange(parts, SRC), *rest_of(near))

    a, b = summed_halves(parts)
    weights = of_device(inverse_weights(16), dev), of_device(last_weights(), dev)
    last = along(mine[3], "core", 1)
    b_far, a_near, last, weights = together(along(b, "xh", 1), around([a] * 4, "z"), last, weights)
    a_near, b_near = jnp.stack(a_near), jnp.stack([b, b_far])
    gathered = [pltpu.with_memory_space_constraint(v, pltpu.HBM) for v in (*mine, *others, last)]
    minus_field = minus_output(dev, gathered, blocks, weights[0])
    a_far, b_all = along(a_near, "xh", 1), around([b_near] * 4, "z")
    a_far, b_all, minus_field = together(a_far, b_all, minus_field)
    a_all, b_all = [a_near, a_far], list(b_all)
    a_all = a_all + [along(v, "core", 1) for v in a_all]
    b_all = b_all + [along(v, "core", 1) for v in b_all]
    plus_field = plus_output(dev, 0, a_all, onsets, focus_start, weights[1], None)
    plus_field = plus_output(dev, 1, b_all, onsets, focus_start, weights[1], plus_field)
    return minus_field, plus_field


def solution(mesh):
    cut = Mesh(mesh.devices.reshape(4, 2, 2, 4, 2), FREQ + SRC)
    return jax.shard_map(
        local,
        mesh=cut,
        in_specs=(P(None, FREQ, None, SRC), P(FREQ, SRC, None), P(SRC, None)),
        out_specs=(P(FREQ, SRC, None), P(FREQ, SRC, None)),
        check_vma=False,
    )
```

```python
import functools
import math

import jax
import jax.numpy as jnp
import ml_dtypes
import numpy as np
from jax import lax
from jax.experimental import pallas as pl
from jax.experimental.pallas import tpu as pltpu
from jax.sharding import Mesh
from jax.sharding import PartitionSpec as P

NT = 256
NF = 16
FREQ = ("z", "xh", "core")
SRC = ("y", "xl")
MIB = 1 << 20


def angle_tables():
    phases = ((np.arange(NF)[:, None] + 1) * np.arange(NT)[None, :]) % NT
    angles = phases.astype(np.float32) * np.float32(2.0 * math.pi / NT)
    return np.cos(angles), np.sin(angles)


def forward_table():
    cosines, sines = angle_tables()
    return np.stack([cosines, -sines], axis=1)


def inverse_table():
    cosines, sines = angle_tables()
    return (2.0 / NT) * np.stack([cosines, -sines], axis=1).reshape(2 * NF, NT).T


def spread(table, rows):
    return np.kron(table, np.eye(rows, dtype=np.float32)).astype(ml_dtypes.bfloat16)


def place(dev):
    return dev // 4, dev // 2 % 2, dev % 2


def frequency(z, xh, core):
    return (z % 4 * 2 + xh % 2) * 2 + core % 2


def first_weights():
    table = forward_table()
    blocks = []
    for dev in range(16):
        z, xh, core = place(dev)
        own = np.arange(dev * 16, dev * 16 + 16)
        other = np.arange((dev ^ 1) * 16, (dev ^ 1) * 16 + 16)
        freqs = [frequency(z + dz, xh + e, core) for dz in range(4) for e in range(2)]
        part = table[freqs].reshape(16, NT)
        blocks.append(spread(part[:, np.concatenate([own, other])], 16))
    return np.stack(blocks)


def last_weights():
    table = inverse_table().reshape(NT, NF, 2)
    blocks = []
    for dev in range(16):
        z, xh, core = place(dev)
        own = np.arange(dev * 16, dev * 16 + 16)
        freqs = [frequency(z - k, xh + e, core + c) for c in range(2) for e in range(2) for k in range(4)]
        blocks.append(spread(table[own][:, freqs].reshape(16, 2 * NF), 16))
    return np.stack(blocks)


def inverse_weights(chunk):
    table = inverse_table()
    return np.stack([spread(table[i : i + chunk], 8) for i in range(0, NT, chunk)])


def forward_weights(chunk):
    table = forward_table().reshape(2 * NF, NT)
    return np.stack([spread(table[:, i : i + chunk], 8) for i in range(0, NT, chunk)])


RESIDENT = pl.BlockSpec(memory_space=pltpu.VMEM)


def resident(*arrays):
    return [pltpu.with_memory_space_constraint(array, pltpu.VMEM) for array in arrays]


def dot(a, b):
    return jnp.dot(a, b, preferred_element_type=jnp.float32)


def params(mib=16):
    return pltpu.CompilerParams(vmem_limit_bytes=mib * MIB)


def cost(flops, moved):
    return pl.CostEstimate(flops=flops, bytes_accessed=moved, transcendentals=0)


HALF = 320


def of_device(table, dev):
    return lax.dynamic_index_in_dim(jnp.asarray(table), dev[0], 0, keepdims=False)


def first_kernel(half, by_z, x_ref, xo_ref, w_ref, *out_refs):
    for at in range(0, HALF, 32):
        sides = []
        for first in (half * HALF + at, half * HALF + at + 16):
            here = slice(first, first + 16)
            both = [x_ref[:, here, :].reshape(256, 128), xo_ref[:, here, :].reshape(256, 128)]
            sides.append(jnp.concatenate(both, axis=0))
        both = dot(w_ref[...], jnp.concatenate(sides, axis=1)).astype(jnp.bfloat16)
        for side in range(2):
            part = both[:, side * 128 : side * 128 + 128].reshape(4, 2, 2, 16, 128)
            here = slice(at + side * 16, at + side * 16 + 16)
            for i, out_ref in enumerate(out_refs):
                out_ref[:, :, here, :] = part[i] if by_z else part[:, i]


def first_transform(weights, x, xo, half, by_z):
    count, lead = (4, 2) if by_z else (2, 4)
    return pl.pallas_call(
        functools.partial(first_kernel, half, by_z),
        out_shape=[pltpu.VMEM((lead, 2, HALF, 128), jnp.bfloat16)] * count,
        in_specs=[RESIDENT] * 3,
        out_specs=[RESIDENT] * count,
        compiler_params=params(),
        cost_estimate=cost(700 << 20, 6 << 20),
        name="first_transform",
    )(*resident(x, xo, weights))


def total_of(refs):
    total = refs[0][...].astype(jnp.float32)
    for ref in refs[1:]:
        total = total + ref[...].astype(jnp.float32)
    return total


def hold(held, real, imag, sign):
    depth = real.shape[0]
    held[:depth, :128] = real.astype(jnp.bfloat16)
    held[:depth, 128:] = imag.astype(jnp.bfloat16)
    held[depth:, :128] = (-sign * imag).astype(jnp.bfloat16)
    held[depth:, 128:] = (sign * real).astype(jnp.bfloat16)


def start_product_kernel(counts, *refs):
    s_refs, (r_ref, out_ref, held) = refs[: sum(counts)], refs[sum(counts) :]

    halves = [total_of(s_refs[: counts[0]]), total_of(s_refs[counts[0] :])]
    real, imag = [jnp.concatenate([h[i] for h in halves], axis=0) for i in range(2)]
    hold(held, real, imag, 1.0)

    def body(i, carry):
        rows = pl.ds(pl.multiple_of(i * 1280, 1280), 1280)
        both = jnp.concatenate([r_ref[0, 0, rows, :], r_ref[1, 0, rows, :]], axis=1)
        part = dot(both, held[...])
        for g in range(32):
            here = slice(g * 40, g * 40 + 40)
            out_ref[i * 32 + g, 0] = part[here, :128].astype(jnp.bfloat16)
            out_ref[i * 32 + g, 1] = part[here, 128:].astype(jnp.bfloat16)
        return carry

    lax.fori_loop(0, 4, body, 0)


def start_product(spectra, counts, reflection):
    depth = reflection.shape[3]
    return pl.pallas_call(
        functools.partial(start_product_kernel, counts),
        out_shape=pltpu.VMEM((128, 2, 40, 128), jnp.bfloat16),
        in_specs=[RESIDENT] * (len(spectra) + 1),
        out_specs=RESIDENT,
        scratch_shapes=[pltpu.VMEM((2 * depth, 256), jnp.bfloat16)],
        compiler_params=params(),
        cost_estimate=cost(4 << 30, 18 << 20),
        name="start_product",
    )(*resident(*spectra, reflection))


def minus_product_kernel(s_ref, r_ref, here_ref, far_ref, out_ref, near_ref, held):
    @pl.when(pl.program_id(0) == 0)
    def _():
        near_ref[0] = here_ref[...]
        near_ref[1] = far_ref[...]
        real, imag = [
            jnp.concatenate([s_ref[i, part].astype(jnp.float32) for i in range(16)], axis=0) for part in range(2)
        ]
        hold(held, real, imag, -1.0)

    rows = pl.ds(pl.multiple_of(pl.program_id(0) * 1280, 1280), 1280)
    both = jnp.concatenate([r_ref[0, 0, rows, :], r_ref[1, 0, rows, :]], axis=1)
    part = dot(both, held[...]).astype(jnp.bfloat16)
    for g in range(out_ref.shape[0]):
        for i in range(2):
            out_ref[g, i] = part[g * 640 : g * 640 + 640, i * 128 : i * 128 + 128]


def minus_product(spectra, reflection, here, far):
    depth = reflection.shape[3]
    rows = 1280
    return pl.pallas_call(
        minus_product_kernel,
        out_shape=[pltpu.HBM((8, 2, 640, 128), jnp.bfloat16), pltpu.HBM((2,) + here.shape, jnp.bfloat16)],
        grid=(5120 // rows,),
        in_specs=[
            RESIDENT,
            RESIDENT,
            RESIDENT,
            RESIDENT,
        ],
        out_specs=[pl.BlockSpec((rows // 640, 2, 640, 128), lambda i: (i, 0, 0, 0)),
            pl.BlockSpec((2,) + here.shape, lambda i: (0, 0, 0, 0)),
        ],
        scratch_shapes=[pltpu.VMEM((2 * depth, 256), jnp.bfloat16)],
        compiler_params=params(),
        cost_estimate=cost(4 << 30, 18 << 20),
        name="minus_product",
    )(*resident(spectra, reflection, here, far))


def sum_kernel(p_ref, a_ref, b_ref):
    total = p_ref[0].astype(jnp.float32)
    for i in range(1, 8):
        total = total + p_ref[i].astype(jnp.float32)
    total = total.astype(jnp.bfloat16)
    a_ref[...] = total[:, :HALF]
    b_ref[...] = total[:, HALF:]


def summed_halves(parts):
    return pl.pallas_call(
        sum_kernel,
        out_shape=[jax.ShapeDtypeStruct((2, HALF, 128), jnp.bfloat16)] * 2,
        grid=(2,),
        in_specs=[pl.BlockSpec((8, 1, 640, 128), lambda i: (0, i, 0, 0))],
        out_specs=[pl.BlockSpec((1, HALF, 128), lambda i: (i, 0, 0))] * 2,
        compiler_params=params(),
        cost_estimate=cost(1 << 20, 3 << 20),
        name="summed_halves",
    )(parts)


def lanes(rows):
    return jnp.concatenate([rows[:, i : i + 8, :].reshape(-1, 128) for i in range(0, 40, 8)], axis=1)


def unlanes(flat):
    parts = [flat[:, i * 128 : i * 128 + 128].reshape(-1, 8, 128) for i in range(5)]
    return jnp.concatenate(parts, axis=1)


def kept(field, first, onsets):
    chunk = field.shape[0] // 8
    times = first + lax.broadcasted_iota(jnp.int32, (chunk, 8, 128), 0)
    distance = jnp.minimum(times, NT - times)
    parts = []
    for i in range(5):
        piece = field[:, i * 128 : i * 128 + 128].reshape(chunk, 8, 128)
        parts.append(jnp.where(distance < onsets[i * 8 : i * 8 + 8][None], piece, 0.0).reshape(-1, 128))
    return jnp.concatenate(parts, axis=1)


def summed_product(p_ref):
    total = p_ref[0].astype(jnp.float32)
    for i in range(1, 8):
        total = total + p_ref[i].astype(jnp.float32)
    return total.reshape(2 * NF, 40, 128)


def middle_kernel(p_ref, onset_ref, wi_ref, wf_ref, sum_ref, out_ref, acc):
    total = summed_product(p_ref)
    sum_ref[...] = total.astype(jnp.bfloat16)
    flat = lanes(total).astype(jnp.bfloat16)
    onsets = onset_ref[0]
    acc[...] = jnp.zeros_like(acc)

    def body(i, carry):
        field = dot(wi_ref[i], flat)
        minus = kept(field, i * 64, onsets).astype(jnp.bfloat16)
        acc[...] += dot(wf_ref[i], minus)
        return carry

    lax.fori_loop(0, 4, body, 0)
    out_ref[...] = unlanes(acc[...]).astype(jnp.bfloat16).reshape(NF, 2, 40, 128)


def onset_spec():
    return pl.BlockSpec((1, 40, 128), lambda i, d: (d[0], 0, 0))


def whole(shape):
    zeros = (0,) * len(shape)
    return pl.BlockSpec(shape, lambda i, d: zeros)


def middle(dev, parts, onsets):
    wi = jnp.asarray(inverse_weights(64))
    wf = jnp.asarray(forward_weights(64))
    return pl.pallas_call(
        lambda d, *refs: middle_kernel(*refs),
        out_shape=(
            pltpu.VMEM((2 * NF, 40, 128), jnp.bfloat16),
            pltpu.VMEM((NF, 2, 40, 128), jnp.bfloat16),
        ),
        grid_spec=pltpu.PrefetchScalarGridSpec(
            num_scalar_prefetch=1,
            grid=(1,),
            in_specs=[RESIDENT, onset_spec(), RESIDENT, RESIDENT],
            out_specs=(RESIDENT, RESIDENT),
            scratch_shapes=[pltpu.VMEM((256, 640), jnp.float32)],
        ),
        compiler_params=params(),
        cost_estimate=cost(2 << 30, 8 << 20),
        name="middle",
    )(dev, *resident(parts), onsets, *resident(wi, wf))


def minus_kernel(dev_ref, *refs):
    p_refs, onset_ref, w_ref, out_ref = refs[:8], refs[8], refs[9], refs[10]
    dev = dev_ref[0]
    z, xh, core = lax.div(dev, 4), lax.rem(lax.div(dev, 2), 2), lax.rem(dev, 2)
    for k in range(4):
        for e in range(2):
            chip = lax.rem(z + 4 - k, 4) * 2 + lax.rem(xh + e, 2)
            pieces = []
            for c, at in ((0, core), (1, 1 - core)):
                flat = lanes(p_refs[c * 4 + k][e].astype(jnp.float32)).astype(jnp.bfloat16)
                pieces.append(unlanes(kept(dot(w_ref[...], flat), dev * 16, onset_ref[chip * 2 + at])))
            swap = core == 1
            both = [jnp.where(swap, pieces[1], pieces[0]), jnp.where(swap, pieces[0], pieces[1])]
            rows = pl.ds(pl.multiple_of(chip * 80, 16), 80)
            out_ref[:, rows, :] = jnp.concatenate(both, axis=1).astype(jnp.bfloat16)


def minus_output(dev, parts, onsets, weights):
    return pl.pallas_call(
        minus_kernel,
        out_shape=jax.ShapeDtypeStruct((16, 640, 128), jnp.bfloat16),
        grid_spec=pltpu.PrefetchScalarGridSpec(
            num_scalar_prefetch=1,
            grid=(1,),
            in_specs=[whole((2, 2 * NF, 40, 128))] * 8
            + [whole((16, 40, 128)), whole((128, 256))],
            out_specs=whole((16, 640, 128)),
        ),
        compiler_params=params(),
        cost_estimate=cost(700 << 20, 8 << 20),
        name="minus_output",
    )(dev, *[pltpu.with_memory_space_constraint(v, pltpu.HBM) for v in parts], onsets, weights)


def plus_kernel(half, dev_ref, *refs):
    *p_refs, onset_ref, x_ref, w_ref = refs[:-2] if half else refs[:-1]
    out_ref = refs[-1]
    first = dev_ref[0] * 16
    rows = x_ref.shape[1]
    times = first + lax.broadcasted_iota(jnp.int32, (16, 16, 128), 0)
    distance = jnp.minimum(times, NT - times)
    done = pl.program_id(0) * rows
    for at in range(0, rows, 32):
        sides = []
        for from_row in (at, at + 16):
            here = pl.ds(pl.multiple_of(done + from_row, 16), 16)
            if half:
                flat = [p_refs[c * 4 + k][e, :, here, :] for c in range(2) for e in range(2) for k in range(4)]
            else:
                flat = [p_refs[c * 2 + e][k, :, here, :] for c in range(2) for e in range(2) for k in range(4)]
            sides.append(jnp.concatenate([piece.reshape(32, 128) for piece in flat], axis=0))
        field = dot(w_ref[...], jnp.concatenate(sides, axis=1))
        for i in range(2):
            here = slice(at + i * 16, at + i * 16 + 16)
            side = field[:, i * 128 : i * 128 + 128].reshape(16, 16, 128)
            update = jnp.where(distance < onset_ref[here][None], side, 0.0)
            out_ref[:, here, :] = (x_ref[:, here, :].astype(jnp.float32) + update).astype(jnp.bfloat16)


def plus_output(dev, half, parts, onsets, x, weights, held):
    step = 160
    start = half * HALF // step
    time_spec = pl.BlockSpec((16, step, 128), lambda i, d: (0, i + start, 0))
    operands = [dev, *resident(*parts), onsets, x, weights] + ([held] if half else [])
    return pl.pallas_call(
        functools.partial(plus_kernel, half),
        out_shape=jax.ShapeDtypeStruct(x.shape, jnp.bfloat16),
        grid_spec=pltpu.PrefetchScalarGridSpec(
            num_scalar_prefetch=1,
            grid=(HALF // step,),
            in_specs=[RESIDENT] * len(parts)
            + [
                pl.BlockSpec((step, 128), lambda i, d: (i + start, 0)),
                time_spec,
                whole((256, 512)),
            ]
            + ([pl.BlockSpec(memory_space=pl.ANY)] if half else []),
            out_specs=time_spec,
        ),
        input_output_aliases={len(operands) - 1: 0} if half else {},
        compiler_params=params(),
        cost_estimate=cost(700 << 20, 6 << 20),
        name="plus_output",
    )(*operands)


def exchange(x, axes):
    return lax.all_to_all(x, axes, 0, 0, tiled=True)


def along(x, axis, step):
    size = lax.axis_size(axis)
    return lax.ppermute(x, axis, [(i, (i + step) % size) for i in range(size)])


def add(*arrays):
    total = arrays[0].astype(jnp.float32)
    for array in arrays[1:]:
        total = total + array.astype(jnp.float32)
    return total.astype(jnp.bfloat16)


STEPS = (2, 1, 3)


def start_spectra(dev, x):
    weights = of_device(first_weights(), dev)
    xo = along(x, "core", 1)
    a_send = first_transform(weights, x, xo, 0, True)
    a_send, xo = together(a_send, xo)
    a_got = around(a_send, "z")
    b_own, b_send = first_transform(weights, x, xo, 1, False)
    b_got = along(b_send, "xh", 1)
    a_got, b_got = together(a_got, b_got)
    a_keep, a_pass = [add(*[got[e] for got in a_got]) for e in range(2)]
    b_parts = around([add(b_own[k], b_got[k]) for k in range(4)], "z")
    return [a_keep, along(a_pass, "xh", 1)] + b_parts


def around(parts, axis):
    got = {k: along(parts[k], axis, k) for k in STEPS}
    return [parts[0], got[1], got[2], got[3]]


def rest_of(near):
    mine = around([near] * 4, "z")
    return mine, [along(v, "core", 1) for v in mine[:3]]


def together(*groups):
    return lax.optimization_barrier(groups)


def local(reflection, focus_start, onsets):
    dev = lax.axis_index(FREQ).astype(jnp.int32).reshape(1)
    blocks = onsets.reshape(16, 40, 128)
    spectra = start_spectra(dev, focus_start)
    start_parts = exchange(start_product(spectra, (2, 4), reflection), SRC + FREQ)
    summed, spectra = middle(dev, start_parts.reshape(8, NF, 2, 40, 128), blocks)
    spectra, far = together(exchange(spectra, FREQ), along(summed, "xh", 1))
    parts, near = minus_product(spectra, reflection, summed, far)
    parts, mine, others = together(exchange(parts, SRC), *rest_of(near))

    a, b = summed_halves(parts)
    weights = of_device(inverse_weights(16), dev), of_device(last_weights(), dev)
    last = along(mine[3], "core", 1)
    b_far, a_near, last, weights = together(along(b, "xh", 1), around([a] * 4, "z"), last, weights)
    a_near, b_near = jnp.stack(a_near), jnp.stack([b, b_far])
    minus_field = minus_output(dev, [*mine, *others, last], blocks, weights[0])
    a_far, b_all = along(a_near, "xh", 1), around([b_near] * 4, "z")
    a_far, b_all, minus_field = together(a_far, b_all, minus_field)
    a_all, b_all = [a_near, a_far], list(b_all)
    a_all = a_all + [along(v, "core", 1) for v in a_all]
    b_all = b_all + [along(v, "core", 1) for v in b_all]
    plus_field = plus_output(dev, 0, a_all, onsets, focus_start, weights[1], None)
    plus_field = plus_output(dev, 1, b_all, onsets, focus_start, weights[1], plus_field)
    return minus_field, plus_field


def solution(mesh):
    cut = Mesh(mesh.devices.reshape(4, 2, 2, 4, 2), FREQ + SRC)
    return jax.shard_map(
        local,
        mesh=cut,
        in_specs=(P(None, FREQ, None, SRC), P(FREQ, SRC, None), P(SRC, None)),
        out_specs=(P(FREQ, SRC, None), P(FREQ, SRC, None)),
        check_vma=False,
    )
```

```python
import functools
import math

import jax
import jax.numpy as jnp
import ml_dtypes
import numpy as np
from jax import lax
from jax.experimental import pallas as pl
from jax.experimental.pallas import tpu as pltpu
from jax.sharding import Mesh
from jax.sharding import PartitionSpec as P

NT = 256
NF = 16
FREQ = ("z", "xh", "core")
SRC = ("y", "xl")
MIB = 1 << 20


def angle_tables():
    phases = ((np.arange(NF)[:, None] + 1) * np.arange(NT)[None, :]) % NT
    angles = phases.astype(np.float32) * np.float32(2.0 * math.pi / NT)
    return np.cos(angles), np.sin(angles)


def forward_table():
    cosines, sines = angle_tables()
    return np.stack([cosines, -sines], axis=1)


def inverse_table():
    cosines, sines = angle_tables()
    return (2.0 / NT) * np.stack([cosines, -sines], axis=1).reshape(2 * NF, NT).T


def spread(table, rows):
    return np.kron(table, np.eye(rows, dtype=np.float32)).astype(ml_dtypes.bfloat16)


def place(dev):
    return dev // 4, dev // 2 % 2, dev % 2


def frequency(z, xh, core):
    return (z % 4 * 2 + xh % 2) * 2 + core % 2


def first_weights():
    table = forward_table()
    blocks = []
    for dev in range(16):
        z, xh, core = place(dev)
        own = np.arange(dev * 16, dev * 16 + 16)
        other = np.arange((dev ^ 1) * 16, (dev ^ 1) * 16 + 16)
        freqs = [frequency(z + dz, xh + e, core) for dz in range(4) for e in range(2)]
        part = table[freqs].reshape(16, NT)
        blocks.append(spread(part[:, np.concatenate([own, other])], 16))
    return np.stack(blocks)


def last_weights():
    table = inverse_table().reshape(NT, NF, 2)
    blocks = []
    for dev in range(16):
        z, xh, core = place(dev)
        own = np.arange(dev * 16, dev * 16 + 16)
        freqs = [frequency(z - k, xh + e, core + c) for c in range(2) for e in range(2) for k in range(4)]
        blocks.append(spread(table[own][:, freqs].reshape(16, 2 * NF), 16))
    return np.stack(blocks)


def inverse_weights(chunk):
    table = inverse_table()
    return np.stack([spread(table[i : i + chunk], 8) for i in range(0, NT, chunk)])


def forward_weights(chunk):
    table = forward_table().reshape(2 * NF, NT)
    return np.stack([spread(table[:, i : i + chunk], 8) for i in range(0, NT, chunk)])


RESIDENT = pl.BlockSpec(memory_space=pltpu.VMEM)


def resident(*arrays):
    return [pltpu.with_memory_space_constraint(array, pltpu.VMEM) for array in arrays]


def dot(a, b):
    return jnp.dot(a, b, preferred_element_type=jnp.float32)


def params(mib=16):
    return pltpu.CompilerParams(vmem_limit_bytes=mib * MIB)


def cost(flops, moved):
    return pl.CostEstimate(flops=flops, bytes_accessed=moved, transcendentals=0)


HALF = 320


def of_device(table, dev):
    return lax.dynamic_index_in_dim(jnp.asarray(table), dev[0], 0, keepdims=False)


def first_kernel(half, by_z, x_ref, xo_ref, w_ref, *out_refs):
    for at in range(0, HALF, 32):
        sides = []
        for first in (half * HALF + at, half * HALF + at + 16):
            here = slice(first, first + 16)
            both = [x_ref[:, here, :].reshape(256, 128), xo_ref[:, here, :].reshape(256, 128)]
            sides.append(jnp.concatenate(both, axis=0))
        both = dot(w_ref[...], jnp.concatenate(sides, axis=1)).astype(jnp.bfloat16)
        for side in range(2):
            part = both[:, side * 128 : side * 128 + 128].reshape(4, 2, 2, 16, 128)
            here = slice(at + side * 16, at + side * 16 + 16)
            for i, out_ref in enumerate(out_refs):
                out_ref[:, :, here, :] = part[i] if by_z else part[:, i]


def first_transform(weights, x, xo, half, by_z):
    count, lead = (4, 2) if by_z else (2, 4)
    return pl.pallas_call(
        functools.partial(first_kernel, half, by_z),
        out_shape=[pltpu.VMEM((lead, 2, HALF, 128), jnp.bfloat16)] * count,
        in_specs=[RESIDENT] * 3,
        out_specs=[RESIDENT] * count,
        compiler_params=params(),
        cost_estimate=cost(700 << 20, 6 << 20),
        name="first_transform",
    )(*resident(x, xo, weights))


def total_of(refs):
    total = refs[0][...].astype(jnp.float32)
    for ref in refs[1:]:
        total = total + ref[...].astype(jnp.float32)
    return total


def hold(held, real, imag, sign):
    depth = real.shape[0]
    held[:depth, :128] = real.astype(jnp.bfloat16)
    held[:depth, 128:] = imag.astype(jnp.bfloat16)
    held[depth:, :128] = (-sign * imag).astype(jnp.bfloat16)
    held[depth:, 128:] = (sign * real).astype(jnp.bfloat16)


def start_product_kernel(counts, *refs):
    s_refs, (r_ref, out_ref, held) = refs[: sum(counts)], refs[sum(counts) :]

    halves = [total_of(s_refs[: counts[0]]), total_of(s_refs[counts[0] :])]
    real, imag = [jnp.concatenate([h[i] for h in halves], axis=0) for i in range(2)]
    hold(held, real, imag, 1.0)

    def body(i, carry):
        rows = pl.ds(pl.multiple_of(i * 1280, 1280), 1280)
        both = jnp.concatenate([r_ref[0, 0, rows, :], r_ref[1, 0, rows, :]], axis=1)
        part = dot(both, held[...])
        for g in range(32):
            here = slice(g * 40, g * 40 + 40)
            out_ref[i * 32 + g, 0] = part[here, :128].astype(jnp.bfloat16)
            out_ref[i * 32 + g, 1] = part[here, 128:].astype(jnp.bfloat16)
        return carry

    lax.fori_loop(0, 4, body, 0)


def start_product(spectra, counts, reflection):
    depth = reflection.shape[3]
    return pl.pallas_call(
        functools.partial(start_product_kernel, counts),
        out_shape=pltpu.VMEM((128, 2, 40, 128), jnp.bfloat16),
        in_specs=[RESIDENT] * (len(spectra) + 1),
        out_specs=RESIDENT,
        scratch_shapes=[pltpu.VMEM((2 * depth, 256), jnp.bfloat16)],
        compiler_params=params(),
        cost_estimate=cost(4 << 30, 18 << 20),
        name="start_product",
    )(*resident(*spectra, reflection))


def minus_product_kernel(s_ref, r_ref, here_ref, far_ref, out_ref, near_ref, held):
    @pl.when(pl.program_id(0) == 0)
    def _():
        near_ref[0] = here_ref[...]
        near_ref[1] = far_ref[...]
        real, imag = [
            jnp.concatenate([s_ref[i, part].astype(jnp.float32) for i in range(16)], axis=0) for part in range(2)
        ]
        hold(held, real, imag, -1.0)

    rows = pl.ds(pl.multiple_of(pl.program_id(0) * 1280, 1280), 1280)
    both = jnp.concatenate([r_ref[0, 0, rows, :], r_ref[1, 0, rows, :]], axis=1)
    part = dot(both, held[...]).astype(jnp.bfloat16)
    for g in range(out_ref.shape[0]):
        for i in range(2):
            out_ref[g, i] = part[g * 640 : g * 640 + 640, i * 128 : i * 128 + 128]


def minus_product(spectra, reflection, here, far):
    depth = reflection.shape[3]
    rows = 1280
    return pl.pallas_call(
        minus_product_kernel,
        out_shape=[pltpu.HBM((8, 2, 640, 128), jnp.bfloat16), pltpu.HBM((2,) + here.shape, jnp.bfloat16)],
        grid=(5120 // rows,),
        in_specs=[
            RESIDENT,
            RESIDENT,
            RESIDENT,
            RESIDENT,
        ],
        out_specs=[pl.BlockSpec((rows // 640, 2, 640, 128), lambda i: (i, 0, 0, 0)),
            pl.BlockSpec((2,) + here.shape, lambda i: (0, 0, 0, 0)),
        ],
        scratch_shapes=[pltpu.VMEM((2 * depth, 256), jnp.bfloat16)],
        compiler_params=params(),
        cost_estimate=cost(4 << 30, 18 << 20),
        name="minus_product",
    )(*resident(spectra, reflection, here, far))


def sum_kernel(p_ref, *refs):
    a_ref, b_ref = refs[-2:]
    total = p_ref[0].astype(jnp.float32)
    for i in range(1, 8):
        total = total + p_ref[i].astype(jnp.float32)
    total = total.astype(jnp.bfloat16)
    a_ref[...] = total[:, :HALF]
    b_ref[...] = total[:, HALF:]


def in_hbm(arrays):
    return [pltpu.with_memory_space_constraint(array, pltpu.HBM) for array in arrays]


def summed_halves(parts, after):
    return pl.pallas_call(
        sum_kernel,
        out_shape=[jax.ShapeDtypeStruct((2, HALF, 128), jnp.bfloat16)] * 2,
        grid=(2,),
        in_specs=[pl.BlockSpec((8, 1, 640, 128), lambda i: (0, i, 0, 0))]
        + [pl.BlockSpec(memory_space=pl.ANY)] * len(after),
        out_specs=[pl.BlockSpec((1, HALF, 128), lambda i: (i, 0, 0))] * 2,
        compiler_params=params(),
        cost_estimate=cost(1 << 20, 3 << 20),
        name="summed_halves",
    )(parts, *in_hbm(after))


def lanes(rows):
    return jnp.concatenate([rows[:, i : i + 8, :].reshape(-1, 128) for i in range(0, 40, 8)], axis=1)


def unlanes(flat):
    parts = [flat[:, i * 128 : i * 128 + 128].reshape(-1, 8, 128) for i in range(5)]
    return jnp.concatenate(parts, axis=1)


def kept(field, first, onsets):
    chunk = field.shape[0] // 8
    times = first + lax.broadcasted_iota(jnp.int32, (chunk, 8, 128), 0)
    distance = jnp.minimum(times, NT - times)
    parts = []
    for i in range(5):
        piece = field[:, i * 128 : i * 128 + 128].reshape(chunk, 8, 128)
        parts.append(jnp.where(distance < onsets[i * 8 : i * 8 + 8][None], piece, 0.0).reshape(-1, 128))
    return jnp.concatenate(parts, axis=1)


def summed_product(p_ref):
    total = p_ref[0].astype(jnp.float32)
    for i in range(1, 8):
        total = total + p_ref[i].astype(jnp.float32)
    return total.reshape(2 * NF, 40, 128)


def middle_kernel(p_ref, onset_ref, wi_ref, wf_ref, sum_ref, out_ref, acc):
    total = summed_product(p_ref)
    sum_ref[...] = total.astype(jnp.bfloat16)
    flat = lanes(total).astype(jnp.bfloat16)
    onsets = onset_ref[0]
    acc[...] = jnp.zeros_like(acc)

    def body(i, carry):
        field = dot(wi_ref[i], flat)
        minus = kept(field, i * 128, onsets).astype(jnp.bfloat16)
        acc[...] += dot(wf_ref[i], minus)
        return carry

    lax.fori_loop(0, 2, body, 0)
    out_ref[...] = unlanes(acc[...]).astype(jnp.bfloat16).reshape(NF, 2, 40, 128)


def onset_spec():
    return pl.BlockSpec((1, 40, 128), lambda i, d: (d[0], 0, 0))


def whole(shape):
    zeros = (0,) * len(shape)
    return pl.BlockSpec(shape, lambda i, d: zeros)


def middle(dev, parts, onsets):
    wi = jnp.asarray(inverse_weights(128))
    wf = jnp.asarray(forward_weights(128))
    return pl.pallas_call(
        lambda d, *refs: middle_kernel(*refs),
        out_shape=(
            pltpu.VMEM((2 * NF, 40, 128), jnp.bfloat16),
            pltpu.VMEM((NF, 2, 40, 128), jnp.bfloat16),
        ),
        grid_spec=pltpu.PrefetchScalarGridSpec(
            num_scalar_prefetch=1,
            grid=(1,),
            in_specs=[RESIDENT, onset_spec(), RESIDENT, RESIDENT],
            out_specs=(RESIDENT, RESIDENT),
            scratch_shapes=[pltpu.VMEM((256, 640), jnp.float32)],
        ),
        compiler_params=params(),
        cost_estimate=cost(2 << 30, 8 << 20),
        name="middle",
    )(dev, *resident(parts), onsets, *resident(wi, wf))


def minus_kernel(dev_ref, *refs):
    p_refs, onset_ref, w_ref, out_ref = refs[:8], refs[8], refs[9], refs[10]
    dev = dev_ref[0]
    z, xh, core = lax.div(dev, 4), lax.rem(lax.div(dev, 2), 2), lax.rem(dev, 2)
    for k in range(4):
        for e in range(2):
            chip = lax.rem(z + 4 - k, 4) * 2 + lax.rem(xh + e, 2)
            pieces = []
            for c, at in ((0, core), (1, 1 - core)):
                flat = lanes(p_refs[c * 4 + k][e].astype(jnp.float32)).astype(jnp.bfloat16)
                pieces.append(unlanes(kept(dot(w_ref[...], flat), dev * 16, onset_ref[chip * 2 + at])))
            swap = core == 1
            both = [jnp.where(swap, pieces[1], pieces[0]), jnp.where(swap, pieces[0], pieces[1])]
            rows = pl.ds(pl.multiple_of(chip * 80, 16), 80)
            out_ref[:, rows, :] = jnp.concatenate(both, axis=1).astype(jnp.bfloat16)


def minus_output(dev, parts, onsets, weights):
    return pl.pallas_call(
        minus_kernel,
        out_shape=jax.ShapeDtypeStruct((16, 640, 128), jnp.bfloat16),
        grid_spec=pltpu.PrefetchScalarGridSpec(
            num_scalar_prefetch=1,
            grid=(1,),
            in_specs=[whole((2, 2 * NF, 40, 128))] * 8
            + [whole((16, 40, 128)), whole((128, 256))],
            out_specs=whole((16, 640, 128)),
        ),
        compiler_params=params(),
        cost_estimate=cost(700 << 20, 8 << 20),
        name="minus_output",
    )(dev, *in_hbm(parts), onsets, weights)


def plus_kernel(half, dev_ref, *refs):
    *p_refs, onset_ref, x_ref, w_ref = refs[:-2] if half else refs[:-1]
    out_ref = refs[-1]
    first = dev_ref[0] * 16
    rows = x_ref.shape[1]
    times = first + lax.broadcasted_iota(jnp.int32, (16, 16, 128), 0)
    distance = jnp.minimum(times, NT - times)
    done = pl.program_id(0) * rows
    for at in range(0, rows, 32):
        sides = []
        for from_row in (at, at + 16):
            here = pl.ds(pl.multiple_of(done + from_row, 16), 16)
            if half:
                flat = [p_refs[c * 4 + k][e, :, here, :] for c in range(2) for e in range(2) for k in range(4)]
            else:
                flat = [p_refs[c * 2 + e][k, :, here, :] for c in range(2) for e in range(2) for k in range(4)]
            sides.append(jnp.concatenate([piece.reshape(32, 128) for piece in flat], axis=0))
        field = dot(w_ref[...], jnp.concatenate(sides, axis=1))
        for i in range(2):
            here = slice(at + i * 16, at + i * 16 + 16)
            side = field[:, i * 128 : i * 128 + 128].reshape(16, 16, 128)
            update = jnp.where(distance < onset_ref[here][None], side, 0.0)
            out_ref[:, here, :] = (x_ref[:, here, :].astype(jnp.float32) + update).astype(jnp.bfloat16)


def plus_output(dev, half, parts, onsets, x, weights, held):
    step = 160
    start = half * HALF // step
    time_spec = pl.BlockSpec((16, step, 128), lambda i, d: (0, i + start, 0))
    operands = [dev, *resident(*parts), onsets, x, weights] + ([held] if half else [])
    return pl.pallas_call(
        functools.partial(plus_kernel, half),
        out_shape=jax.ShapeDtypeStruct(x.shape, jnp.bfloat16),
        grid_spec=pltpu.PrefetchScalarGridSpec(
            num_scalar_prefetch=1,
            grid=(HALF // step,),
            in_specs=[RESIDENT] * len(parts)
            + [
                pl.BlockSpec((step, 128), lambda i, d: (i + start, 0)),
                time_spec,
                whole((256, 512)),
            ]
            + ([pl.BlockSpec(memory_space=pl.ANY)] if half else []),
            out_specs=time_spec,
        ),
        input_output_aliases={len(operands) - 1: 0} if half else {},
        compiler_params=params(),
        cost_estimate=cost(700 << 20, 6 << 20),
        name="plus_output",
    )(*operands)


def exchange(x, axes):
    return lax.all_to_all(x, axes, 0, 0, tiled=True)


def along(x, axis, step):
    size = lax.axis_size(axis)
    return lax.ppermute(x, axis, [(i, (i + step) % size) for i in range(size)])


def add(*arrays):
    total = arrays[0].astype(jnp.float32)
    for array in arrays[1:]:
        total = total + array.astype(jnp.float32)
    return total.astype(jnp.bfloat16)


STEPS = (1, 3, 2)


def start_spectra(dev, x):
    weights = of_device(first_weights(), dev)
    xo = along(x, "core", 1)
    a_send = first_transform(weights, x, xo, 0, True)
    a_send, xo = together(a_send, xo)
    a_got = around(a_send, "z")
    b_own, b_send = first_transform(weights, x, xo, 1, False)
    b_got = along(b_send, "xh", 1)
    a_got, b_got = together(a_got, b_got)
    a_keep, a_pass = [add(*[got[e] for got in a_got]) for e in range(2)]
    b_parts = around([add(b_own[k], b_got[k]) for k in range(4)], "z")
    return [a_keep, along(a_pass, "xh", 1)] + b_parts


def around(parts, axis):
    got = {k: along(parts[k], axis, k) for k in STEPS}
    return [parts[0], got[1], got[2], got[3]]


def rest_of(near):
    mine = around([near] * 4, "z")
    return mine, [along(v, "core", 1) for v in mine[:3]]


def together(*groups):
    return lax.optimization_barrier(groups)


def local(reflection, focus_start, onsets):
    dev = lax.axis_index(FREQ).astype(jnp.int32).reshape(1)
    blocks = onsets.reshape(16, 40, 128)
    spectra = start_spectra(dev, focus_start)
    start_parts = exchange(start_product(spectra, (2, 4), reflection), SRC + FREQ)
    summed, spectra = middle(dev, start_parts.reshape(8, NF, 2, 40, 128), blocks)
    spectra, far = together(exchange(spectra, FREQ), along(summed, "xh", 1))
    parts, near = minus_product(spectra, reflection, summed, far)
    parts, (mine, others) = exchange(parts, SRC), rest_of(near)

    a, b = summed_halves(parts, [*mine[1:], *others])
    weights = of_device(inverse_weights(16), dev), of_device(last_weights(), dev)
    last = along(mine[3], "core", 1)
    b_far, a_near, last, weights = together(along(b, "xh", 1), around([a] * 4, "z"), last, weights)
    a_near, b_near = jnp.stack(a_near), jnp.stack([b, b_far])
    minus_field = minus_output(dev, [*mine, *others, last], blocks, weights[0])
    a_far, b_all = along(a_near, "xh", 1), around([b_near] * 4, "z")
    a_far, b_all, minus_field = together(a_far, b_all, minus_field)
    a_all, b_all = [a_near, a_far], list(b_all)
    a_all = a_all + [along(v, "core", 1) for v in a_all]
    b_all = b_all + [along(v, "core", 1) for v in b_all]
    plus_field = plus_output(dev, 0, a_all, onsets, focus_start, weights[1], None)
    plus_field = plus_output(dev, 1, b_all, onsets, focus_start, weights[1], plus_field)
    return minus_field, plus_field


def solution(mesh):
    cut = Mesh(mesh.devices.reshape(4, 2, 2, 4, 2), FREQ + SRC)
    return jax.shard_map(
        local,
        mesh=cut,
        in_specs=(P(None, FREQ, None, SRC), P(FREQ, SRC, None), P(SRC, None)),
        out_specs=(P(FREQ, SRC, None), P(FREQ, SRC, None)),
        check_vma=False,
    )
```

```python
import functools
import math

import jax
import jax.numpy as jnp
import ml_dtypes
import numpy as np
from jax import lax
from jax.experimental import pallas as pl
from jax.experimental.pallas import tpu as pltpu
from jax.sharding import Mesh
from jax.sharding import PartitionSpec as P

NT = 256
NF = 16
FREQ = ("z", "xh", "core")
SRC = ("y", "xl")
MIB = 1 << 20


def angle_tables():
    phases = ((np.arange(NF)[:, None] + 1) * np.arange(NT)[None, :]) % NT
    angles = phases.astype(np.float32) * np.float32(2.0 * math.pi / NT)
    return np.cos(angles), np.sin(angles)


def forward_table():
    cosines, sines = angle_tables()
    return np.stack([cosines, -sines], axis=1)


def inverse_table():
    cosines, sines = angle_tables()
    return (2.0 / NT) * np.stack([cosines, -sines], axis=1).reshape(2 * NF, NT).T


def spread(table, rows):
    return np.kron(table, np.eye(rows, dtype=np.float32)).astype(ml_dtypes.bfloat16)


def place(dev):
    return dev // 4, dev // 2 % 2, dev % 2


def frequency(z, xh, core):
    return (z % 4 * 2 + xh % 2) * 2 + core % 2


def first_weights():
    table = forward_table()
    blocks = []
    for dev in range(16):
        z, xh, core = place(dev)
        own = np.arange(dev * 16, dev * 16 + 16)
        other = np.arange((dev ^ 1) * 16, (dev ^ 1) * 16 + 16)
        freqs = [frequency(z + dz, xh + e, core) for dz in range(4) for e in range(2)]
        part = table[freqs].reshape(16, NT)
        blocks.append(spread(part[:, np.concatenate([own, other])], 16))
    return np.stack(blocks)


def last_weights():
    table = inverse_table().reshape(NT, NF, 2)
    blocks = []
    for dev in range(16):
        z, xh, core = place(dev)
        own = np.arange(dev * 16, dev * 16 + 16)
        freqs = [frequency(z - k, xh + e, core + c) for c in range(2) for e in range(2) for k in range(4)]
        blocks.append(spread(table[own][:, freqs].reshape(16, 2 * NF), 16))
    return np.stack(blocks)


def inverse_weights(chunk):
    table = inverse_table()
    return np.stack([spread(table[i : i + chunk], 8) for i in range(0, NT, chunk)])


def forward_weights(chunk):
    table = forward_table().reshape(2 * NF, NT)
    return np.stack([spread(table[:, i : i + chunk], 8) for i in range(0, NT, chunk)])


RESIDENT = pl.BlockSpec(memory_space=pltpu.VMEM)


def resident(*arrays):
    return [pltpu.with_memory_space_constraint(array, pltpu.VMEM) for array in arrays]


def dot(a, b):
    return jnp.dot(a, b, preferred_element_type=jnp.float32)


def params(mib=16):
    return pltpu.CompilerParams(vmem_limit_bytes=mib * MIB)


def cost(flops, moved):
    return pl.CostEstimate(flops=flops, bytes_accessed=moved, transcendentals=0)


HALF = 320


def of_device(table, dev):
    return lax.dynamic_index_in_dim(jnp.asarray(table), dev[0], 0, keepdims=False)


def first_kernel(half, by_z, x_ref, xo_ref, w_ref, *out_refs):
    for at in range(0, HALF, 32):
        sides = []
        for first in (half * HALF + at, half * HALF + at + 16):
            here = slice(first, first + 16)
            both = [x_ref[:, here, :].reshape(256, 128), xo_ref[:, here, :].reshape(256, 128)]
            sides.append(jnp.concatenate(both, axis=0))
        both = dot(w_ref[...], jnp.concatenate(sides, axis=1)).astype(jnp.bfloat16)
        for side in range(2):
            part = both[:, side * 128 : side * 128 + 128].reshape(4, 2, 2, 16, 128)
            here = slice(at + side * 16, at + side * 16 + 16)
            for i, out_ref in enumerate(out_refs):
                out_ref[:, :, here, :] = part[i] if by_z else part[:, i]


def first_transform(weights, x, xo, half, by_z):
    count, lead = (4, 2) if by_z else (2, 4)
    return pl.pallas_call(
        functools.partial(first_kernel, half, by_z),
        out_shape=[pltpu.VMEM((lead, 2, HALF, 128), jnp.bfloat16)] * count,
        in_specs=[RESIDENT] * 3,
        out_specs=[RESIDENT] * count,
        compiler_params=params(),
        cost_estimate=cost(700 << 20, 6 << 20),
        name="first_transform",
    )(*resident(x, xo, weights))


def total_of(refs):
    total = refs[0][...].astype(jnp.float32)
    for ref in refs[1:]:
        total = total + ref[...].astype(jnp.float32)
    return total


def hold(held, real, imag, sign):
    depth = real.shape[0]
    held[:depth, :128] = real.astype(jnp.bfloat16)
    held[:depth, 128:] = imag.astype(jnp.bfloat16)
    held[depth:, :128] = (-sign * imag).astype(jnp.bfloat16)
    held[depth:, 128:] = (sign * real).astype(jnp.bfloat16)


def start_product_kernel(counts, *refs):
    s_refs, (r_ref, out_ref, held) = refs[: sum(counts)], refs[sum(counts) :]

    halves = [total_of(s_refs[: counts[0]]), total_of(s_refs[counts[0] :])]
    real, imag = [jnp.concatenate([h[i] for h in halves], axis=0) for i in range(2)]
    hold(held, real, imag, 1.0)

    def body(i, carry):
        rows = pl.ds(pl.multiple_of(i * 1280, 1280), 1280)
        both = jnp.concatenate([r_ref[0, 0, rows, :], r_ref[1, 0, rows, :]], axis=1)
        part = dot(both, held[...])
        for g in range(32):
            here = slice(g * 40, g * 40 + 40)
            out_ref[i * 32 + g, 0] = part[here, :128].astype(jnp.bfloat16)
            out_ref[i * 32 + g, 1] = part[here, 128:].astype(jnp.bfloat16)
        return carry

    lax.fori_loop(0, 4, body, 0)


def start_product(spectra, counts, reflection):
    depth = reflection.shape[3]
    return pl.pallas_call(
        functools.partial(start_product_kernel, counts),
        out_shape=pltpu.VMEM((128, 2, 40, 128), jnp.bfloat16),
        in_specs=[RESIDENT] * (len(spectra) + 1),
        out_specs=RESIDENT,
        scratch_shapes=[pltpu.VMEM((2 * depth, 256), jnp.bfloat16)],
        compiler_params=params(),
        cost_estimate=cost(4 << 30, 18 << 20),
        name="start_product",
    )(*resident(*spectra, reflection))


def minus_product_kernel(s_ref, r_ref, here_ref, far_ref, out_ref, near_ref, held):
    @pl.when(pl.program_id(0) == 0)
    def _():
        near_ref[0] = here_ref[...]
        near_ref[1] = far_ref[...]
        real, imag = [
            jnp.concatenate([s_ref[i, part].astype(jnp.float32) for i in range(16)], axis=0) for part in range(2)
        ]
        hold(held, real, imag, -1.0)

    rows = pl.ds(pl.multiple_of(pl.program_id(0) * 1280, 1280), 1280)
    both = jnp.concatenate([r_ref[0, 0, rows, :], r_ref[1, 0, rows, :]], axis=1)
    part = dot(both, held[...]).astype(jnp.bfloat16)
    for g in range(out_ref.shape[0]):
        for i in range(2):
            out_ref[g, i] = part[g * 640 : g * 640 + 640, i * 128 : i * 128 + 128]


def minus_product(spectra, reflection, here, far):
    depth = reflection.shape[3]
    rows = 1280
    return pl.pallas_call(
        minus_product_kernel,
        out_shape=[pltpu.HBM((8, 2, 640, 128), jnp.bfloat16), pltpu.HBM((2,) + here.shape, jnp.bfloat16)],
        grid=(5120 // rows,),
        in_specs=[
            RESIDENT,
            RESIDENT,
            RESIDENT,
            RESIDENT,
        ],
        out_specs=[pl.BlockSpec((rows // 640, 2, 640, 128), lambda i: (i, 0, 0, 0)),
            pl.BlockSpec((2,) + here.shape, lambda i: (0, 0, 0, 0)),
        ],
        scratch_shapes=[pltpu.VMEM((2 * depth, 256), jnp.bfloat16)],
        compiler_params=params(),
        cost_estimate=cost(4 << 30, 18 << 20),
        name="minus_product",
    )(*resident(spectra, reflection, here, far))


def sum_kernel(p_ref, a_ref, b_ref):
    total = p_ref[0].astype(jnp.float32)
    for i in range(1, 8):
        total = total + p_ref[i].astype(jnp.float32)
    total = total.astype(jnp.bfloat16)
    a_ref[...] = total[:, :HALF]
    b_ref[...] = total[:, HALF:]


def summed_halves(parts):
    return pl.pallas_call(
        sum_kernel,
        out_shape=[jax.ShapeDtypeStruct((2, HALF, 128), jnp.bfloat16)] * 2,
        grid=(2,),
        in_specs=[pl.BlockSpec((8, 1, 640, 128), lambda i: (0, i, 0, 0))],
        out_specs=[pl.BlockSpec((1, HALF, 128), lambda i: (i, 0, 0))] * 2,
        compiler_params=params(),
        cost_estimate=cost(1 << 20, 3 << 20),
        name="summed_halves",
    )(parts)


def lanes(rows):
    return jnp.concatenate([rows[:, i : i + 8, :].reshape(-1, 128) for i in range(0, 40, 8)], axis=1)


def unlanes(flat):
    parts = [flat[:, i * 128 : i * 128 + 128].reshape(-1, 8, 128) for i in range(5)]
    return jnp.concatenate(parts, axis=1)


def kept(field, first, onsets):
    chunk = field.shape[0] // 8
    times = first + lax.broadcasted_iota(jnp.int32, (chunk, 8, 128), 0)
    distance = jnp.minimum(times, NT - times)
    parts = []
    for i in range(5):
        piece = field[:, i * 128 : i * 128 + 128].reshape(chunk, 8, 128)
        parts.append(jnp.where(distance < onsets[i * 8 : i * 8 + 8][None], piece, 0.0).reshape(-1, 128))
    return jnp.concatenate(parts, axis=1)


def summed_product(p_ref):
    total = p_ref[0].astype(jnp.float32)
    for i in range(1, 8):
        total = total + p_ref[i].astype(jnp.float32)
    return total.reshape(2 * NF, 40, 128)


def middle_kernel(p_ref, onset_ref, wi_ref, wf_ref, sum_ref, out_ref, acc):
    total = summed_product(p_ref)
    sum_ref[...] = total.astype(jnp.bfloat16)
    flat = lanes(total).astype(jnp.bfloat16)
    onsets = onset_ref[0]
    acc[...] = jnp.zeros_like(acc)

    def body(i, carry):
        field = dot(wi_ref[i], flat)
        minus = kept(field, i * 128, onsets).astype(jnp.bfloat16)
        acc[...] += dot(wf_ref[i], minus)
        return carry

    lax.fori_loop(0, 2, body, 0)
    out_ref[...] = unlanes(acc[...]).astype(jnp.bfloat16).reshape(NF, 2, 40, 128)


def onset_spec():
    return pl.BlockSpec((1, 40, 128), lambda i, d: (d[0], 0, 0))


def whole(shape):
    zeros = (0,) * len(shape)
    return pl.BlockSpec(shape, lambda i, d: zeros)


def middle(dev, parts, onsets):
    wi = jnp.asarray(inverse_weights(128))
    wf = jnp.asarray(forward_weights(128))
    return pl.pallas_call(
        lambda d, *refs: middle_kernel(*refs),
        out_shape=(
            pltpu.VMEM((2 * NF, 40, 128), jnp.bfloat16),
            pltpu.VMEM((NF, 2, 40, 128), jnp.bfloat16),
        ),
        grid_spec=pltpu.PrefetchScalarGridSpec(
            num_scalar_prefetch=1,
            grid=(1,),
            in_specs=[RESIDENT, onset_spec(), RESIDENT, RESIDENT],
            out_specs=(RESIDENT, RESIDENT),
            scratch_shapes=[pltpu.VMEM((256, 640), jnp.float32)],
        ),
        compiler_params=params(),
        cost_estimate=cost(2 << 30, 8 << 20),
        name="middle",
    )(dev, *resident(parts), onsets, *resident(wi, wf))


def minus_kernel(dev_ref, *refs):
    p_refs, onset_ref, w_ref, out_ref = refs[:8], refs[8], refs[9], refs[10]
    dev = dev_ref[0]
    z, xh, core = lax.div(dev, 4), lax.rem(lax.div(dev, 2), 2), lax.rem(dev, 2)
    for k in range(4):
        for e in range(2):
            chip = lax.rem(z + 4 - k, 4) * 2 + lax.rem(xh + e, 2)
            pieces = []
            for c, at in ((0, core), (1, 1 - core)):
                flat = lanes(p_refs[c * 4 + k][e].astype(jnp.float32)).astype(jnp.bfloat16)
                pieces.append(unlanes(kept(dot(w_ref[...], flat), dev * 16, onset_ref[chip * 2 + at])))
            swap = core == 1
            both = [jnp.where(swap, pieces[1], pieces[0]), jnp.where(swap, pieces[0], pieces[1])]
            rows = pl.ds(pl.multiple_of(chip * 80, 16), 80)
            out_ref[:, rows, :] = jnp.concatenate(both, axis=1).astype(jnp.bfloat16)


def minus_output(dev, parts, onsets, weights):
    return pl.pallas_call(
        minus_kernel,
        out_shape=jax.ShapeDtypeStruct((16, 640, 128), jnp.bfloat16),
        grid_spec=pltpu.PrefetchScalarGridSpec(
            num_scalar_prefetch=1,
            grid=(1,),
            in_specs=[whole((2, 2 * NF, 40, 128))] * 8
            + [whole((16, 40, 128)), whole((128, 256))],
            out_specs=whole((16, 640, 128)),
        ),
        compiler_params=params(),
        cost_estimate=cost(700 << 20, 8 << 20),
        name="minus_output",
    )(dev, *[pltpu.with_memory_space_constraint(v, pltpu.HBM) for v in parts], onsets, weights)


def plus_kernel(half, dev_ref, *refs):
    *p_refs, onset_ref, x_ref, w_ref = refs[:-2] if half else refs[:-1]
    out_ref = refs[-1]
    first = dev_ref[0] * 16
    rows = x_ref.shape[1]
    times = first + lax.broadcasted_iota(jnp.int32, (16, 16, 128), 0)
    distance = jnp.minimum(times, NT - times)
    done = pl.program_id(0) * rows
    for at in range(0, rows, 32):
        sides = []
        for from_row in (at, at + 16):
            here = pl.ds(pl.multiple_of(done + from_row, 16), 16)
            if half:
                flat = [p_refs[c * 4 + k][e, :, here, :] for c in range(2) for e in range(2) for k in range(4)]
            else:
                flat = [p_refs[c * 2 + e][k, :, here, :] for c in range(2) for e in range(2) for k in range(4)]
            sides.append(jnp.concatenate([piece.reshape(32, 128) for piece in flat], axis=0))
        field = dot(w_ref[...], jnp.concatenate(sides, axis=1))
        for i in range(2):
            here = slice(at + i * 16, at + i * 16 + 16)
            side = field[:, i * 128 : i * 128 + 128].reshape(16, 16, 128)
            update = jnp.where(distance < onset_ref[here][None], side, 0.0)
            out_ref[:, here, :] = (x_ref[:, here, :].astype(jnp.float32) + update).astype(jnp.bfloat16)


def plus_output(dev, half, parts, onsets, x, weights, held):
    step = 160
    start = half * HALF // step
    time_spec = pl.BlockSpec((16, step, 128), lambda i, d: (0, i + start, 0))
    operands = [dev, *resident(*parts), onsets, x, weights] + ([held] if half else [])
    return pl.pallas_call(
        functools.partial(plus_kernel, half),
        out_shape=jax.ShapeDtypeStruct(x.shape, jnp.bfloat16),
        grid_spec=pltpu.PrefetchScalarGridSpec(
            num_scalar_prefetch=1,
            grid=(HALF // step,),
            in_specs=[RESIDENT] * len(parts)
            + [
                pl.BlockSpec((step, 128), lambda i, d: (i + start, 0)),
                time_spec,
                whole((256, 512)),
            ]
            + ([pl.BlockSpec(memory_space=pl.ANY)] if half else []),
            out_specs=time_spec,
        ),
        input_output_aliases={len(operands) - 1: 0} if half else {},
        compiler_params=params(),
        cost_estimate=cost(700 << 20, 6 << 20),
        name="plus_output",
    )(*operands)


def exchange(x, axes):
    return lax.all_to_all(x, axes, 0, 0, tiled=True)


def along(x, axis, step):
    size = lax.axis_size(axis)
    return lax.ppermute(x, axis, [(i, (i + step) % size) for i in range(size)])


def add(*arrays):
    total = arrays[0].astype(jnp.float32)
    for array in arrays[1:]:
        total = total + array.astype(jnp.float32)
    return total.astype(jnp.bfloat16)


STEPS = (2, 1, 3)


def start_spectra(dev, x):
    weights = of_device(first_weights(), dev)
    xo = along(x, "core", 1)
    a_send = first_transform(weights, x, xo, 0, True)
    a_send, xo = together(a_send, xo)
    a_got = around(a_send, "z")
    b_own, b_send = first_transform(weights, x, xo, 1, False)
    b_got = along(b_send, "xh", 1)
    a_got, b_got = together(a_got, b_got)
    a_keep, a_pass = [add(*[got[e] for got in a_got]) for e in range(2)]
    b_parts = around([add(b_own[k], b_got[k]) for k in range(4)], "z")
    return [a_keep, along(a_pass, "xh", 1)] + b_parts


def around(parts, axis):
    got = {k: along(parts[k], axis, k) for k in STEPS}
    return [parts[0], got[1], got[2], got[3]]


def rest_of(near):
    mine = around([near] * 4, "z")
    return mine, [along(v, "core", 1) for v in mine[:3]]


def together(*groups):
    return lax.optimization_barrier(groups)


def local(reflection, focus_start, onsets):
    dev = lax.axis_index(FREQ).astype(jnp.int32).reshape(1)
    blocks = onsets.reshape(16, 40, 128)
    spectra = start_spectra(dev, focus_start)
    start_parts = exchange(start_product(spectra, (2, 4), reflection), SRC + FREQ)
    summed, spectra = middle(dev, start_parts.reshape(8, NF, 2, 40, 128), blocks)
    spectra, far = together(exchange(spectra, FREQ), along(summed, "xh", 1))
    parts, near = minus_product(spectra, reflection, summed, far)
    parts, mine, others = together(exchange(parts, SRC), *rest_of(near))

    a, b = summed_halves(parts)
    weights = of_device(inverse_weights(16), dev), of_device(last_weights(), dev)
    last = along(mine[3], "core", 1)
    b_far, a_near, last, weights = together(along(b, "xh", 1), around([a] * 4, "z"), last, weights)
    a_near, b_near = jnp.stack(a_near), jnp.stack([b, b_far])
    minus_field = minus_output(dev, [*mine, *others, last], blocks, weights[0])
    a_far, b_all = along(a_near, "xh", 1), around([b_near] * 4, "z")
    a_far, b_all, minus_field = together(a_far, b_all, minus_field)
    a_all, b_all = [a_near, a_far], list(b_all)
    a_all = a_all + [along(v, "core", 1) for v in a_all]
    b_all = b_all + [along(v, "core", 1) for v in b_all]
    plus_field = plus_output(dev, 0, a_all, onsets, focus_start, weights[1], None)
    plus_field = plus_output(dev, 1, b_all, onsets, focus_start, weights[1], plus_field)
    return minus_field, plus_field


def solution(mesh):
    cut = Mesh(mesh.devices.reshape(4, 2, 2, 4, 2), FREQ + SRC)
    return jax.shard_map(
        local,
        mesh=cut,
        in_specs=(P(None, FREQ, None, SRC), P(FREQ, SRC, None), P(SRC, None)),
        out_specs=(P(FREQ, SRC, None), P(FREQ, SRC, None)),
        check_vma=False,
    )
```
